256 devices in a mesh: dp: 8 (over x, core), expert: 32 (over z, y).
Axes of the slice: x: 4, y: 4, z: 8, core: 2. Of those that a mesh axis runs over, the one named last changes fastest.
Arguments:
- tokens: bfloat16 [14336, 2048], P(('dp', 'expert')), may hold values from -6 to 6
- expert_ids: int32 [14336, 8], P(('dp', 'expert')), may hold values from 0 to 31, all different within a row; in each aligned block of 56 rows (0 to 55, 56 to 111, ...) at most 16 rows name the same one
- combine: float32 [14336, 8], P(('dp', 'expert')), may hold values from 0.2 to 1
- w_gate: bfloat16 [32, 2048, 768], P('expert'), may hold values from -0.125 to 0.125
- w_up: bfloat16 [32, 2048, 768], P('expert'), may hold values from -0.125 to 0.125
- w_down: bfloat16 [32, 768, 2048], P('expert'), may hold values from -0.21875 to 0.21875
- grad_out: bfloat16 [14336, 2048], P(('dp', 'expert')), may hold values from -6 to 6
Outputs:
- mixed: bfloat16 [14336, 2048], P(('dp', 'expert'))
- grad_tokens: bfloat16 [14336, 2048], P(('dp', 'expert'))
- grad_gate: bfloat16 [32, 2048, 768], P('expert', 'dp')
- grad_up: bfloat16 [32, 2048, 768], P('expert', 'dp')
- grad_down: bfloat16 [32, 768, 2048], P('expert', None, 'dp')
The draws below stay inside these ranges and needn't reach their ends.
Inputs may be any that keep to these rules, and one draw needn't show every extreme that they name: `expert_ids`: each row names 8 different experts. Within the 56 rows of one device no expert is named by more than 16 rows, and in every draw some expert is named by exactly 16 rows of some device.
All inputs are finite; a program needn't handle non-finite values.
Results may differ from the reference program's by a relative error of at most 0.017.
Values may be sent and summed in bfloat16 or wider, within the bound.
No kernel may reach another device: no remote copies, remote signals or barrier semaphores. Data moves between devices by JAX's collectives and lax.ppermute only.
A program may use at most 128 MiB of HBM per device.

```python
import math
import jax
import jax.numpy as jnp
import numpy as np
from jax import lax

D = 2048
H = 768
TOPK = 8
TOK_DEV = 56
EXPERTS = 32
CAP = 16
TOKENS = 14336
N_DP = 8
N_EXPERT = 32


def levels(rng, dims, split, smallest, high):
    factor_of = 1.0
    for position, shards_of in split:
        heights = jax.random.uniform(jax.random.fold_in(jax.random.fold_in(rng, 6), position), (shards_of,), jnp.float32, smallest / len(split), high / len(split))
        factor_of = factor_of * jnp.repeat(jnp.exp(heights), dims[position] // shards_of).reshape((-1,) + (1,) * (len(dims) - 1 - position))
    return factor_of


def shared_out(key, own, number, rows, amount, top, limit, skew):
    sequence = jax.random.permutation(key, amount)
    packed, usual = portions_of(amount, rows * top, limit, skew, True), portions_of(amount, rows * top, limit, skew, False)
    places = jnp.arange(amount)

    def named(lengths, offset_by):
        used = int((lengths > 0).sum())
        fixed = max(1, used // 4)
        shifted = fixed + (places - fixed + offset_by * (used - fixed)) % max(1, amount - fixed)
        return jnp.zeros((amount,), jnp.int32).at[sequence[jnp.where(places < fixed, places, shifted)]].set(jnp.asarray(lengths, jnp.int32))

    lengths = jnp.where(number % 4 == 0, named(packed, number // 4), named(usual, number - number // 4 - 1))
    mixed = jax.random.permutation(jax.random.fold_in(own, 3), amount)
    donor, sink = mixed[0:amount // 2 * 2:2], mixed[1:amount // 2 * 2:2]
    slack = jnp.minimum(lengths[donor] - 1, limit - lengths[sink]) // 2
    slack = jnp.where((donor == sequence[0]) | (sink == sequence[0]) | (lengths[sink] == 0), 0, jnp.maximum(slack, 0))
    shifted = jax.random.randint(jax.random.fold_in(own, 4), (amount // 2,), 0, 1 << 20) % (slack + 1)
    lengths = lengths.at[donor].add(-shifted).at[sink].add(shifted)
    items = jnp.searchsorted(jnp.cumsum(lengths), jnp.arange(rows * top), side="right").astype(jnp.int32)
    listing = items.reshape(top, rows).T
    listing = listing[jax.random.permutation(jax.random.fold_in(own, 1), rows)]
    offset_by = jax.random.randint(jax.random.fold_in(own, 2), (rows, 1), 0, top)
    return jnp.take_along_axis(listing, (jnp.arange(top)[None, :] + offset_by) % top, axis=1)


def portions_of(number_of, total, bound, slope, full):
    weights = [(1 << 20) // math.isqrt(grade ** slope) + 1 for grade in range(1, number_of + 1)]
    largest = bound if full else min(bound, max(-(-total // number_of), total * weights[0] // sum(weights)))
    least = 1 if total - largest >= number_of - 1 else 0
    given, spare = [largest] + [least] * (number_of - 1), total - largest - least * (number_of - 1)
    while spare > 0:
        movable = [i for i in range(1, number_of) if given[i] < largest] or [i for i in range(1, number_of) if given[i] < bound]
        whole, budget = sum([weights[i] for i in movable]), spare
        for i in movable:
            more = min(bound - given[i], max(1, budget * weights[i] // whole), spare)
            given[i] = given[i] + more
            spare = spare - more
    return np.array(given)


def noise(rng, extent, width, limit, pieces=(), kind=jnp.bfloat16):
    values = width * jax.random.normal(rng, extent, jnp.float32)
    if pieces:
        values = values * levels(rng, extent, pieces, -0.22, 0.18)
    return jnp.clip(values, -limit, limit).astype(kind)


def setup_inputs(seed: int = 0) -> dict:
    splits = jax.random.split(jax.random.key(seed), 8)
    tokens = noise(splits[0], (TOKENS, D), 1.0, 6.0, ((0, 256),))
    expert_ids_keys = jax.random.split(jax.random.fold_in(splits[1], 1), TOKENS // TOK_DEV)
    expert_ids_turns = jax.random.permutation(jax.random.fold_in(splits[1], 3), TOKENS // TOK_DEV)
    expert_ids = jax.vmap(lambda own, number: shared_out(jax.random.fold_in(splits[1], 2), own, number, TOK_DEV, EXPERTS, TOPK, CAP, 1))(expert_ids_keys, expert_ids_turns).reshape((TOKENS, TOPK))
    combine = jnp.clip(0.2 + 0.8 * jax.random.uniform(splits[2], (TOKENS, TOPK), jnp.float32) ** levels(splits[2], (TOKENS, TOPK), ((0, 256),), -0.2, 0.2), 0.2, 1.0)
    w_gate = noise(splits[3], (EXPERTS, D, H), D ** -0.5, 0.125, ((0, 32),))
    w_up = noise(splits[4], (EXPERTS, D, H), D ** -0.5, 0.125, ((0, 32),))
    w_down = noise(splits[5], (EXPERTS, H, D), H ** -0.5, 0.21875, ((0, 32),))
    grad_out = noise(splits[6], (TOKENS, D), 1.0, 6.0, ((0, 256),))
    return {"tokens": tokens, "expert_ids": expert_ids, "combine": combine, "w_gate": w_gate, "w_up": w_up, "w_down": w_down, "grad_out": grad_out}


def slot_table(ids):
    flat = ids.reshape(-1).astype(jnp.int32)
    onehot = (flat[:, None] == jnp.arange(EXPERTS, dtype=jnp.int32)[None, :]).astype(jnp.int32)
    ranks = jnp.sum(jnp.cumsum(onehot, axis=0) * onehot, axis=1) - 1
    return flat, ranks.astype(jnp.int32)


def expert_pass(rows, cotangent, w_gate, w_up, w_down):
    gate = jnp.dot(rows, w_gate, preferred_element_type=jnp.float32)
    upper = jnp.dot(rows, w_up, preferred_element_type=jnp.float32)
    sigma = jax.nn.sigmoid(gate)
    hidden = (gate * sigma * upper).astype(jnp.bfloat16)
    output = jnp.dot(hidden, w_down, preferred_element_type=jnp.float32).astype(jnp.bfloat16)
    d_hidden = lax.dot_general(cotangent, w_down, (((1,), (1,)), ((), ())), preferred_element_type=jnp.float32)
    d_gate = (d_hidden * upper * sigma * (1.0 + gate * (1.0 - sigma))).astype(jnp.bfloat16)
    d_upper = (d_hidden * gate * sigma).astype(jnp.bfloat16)
    d_rows = lax.dot_general(d_gate, w_gate, (((1,), (1,)), ((), ())), preferred_element_type=jnp.float32)
    d_rows = (d_rows + lax.dot_general(d_upper, w_up, (((1,), (1,)), ((), ())), preferred_element_type=jnp.float32)).astype(jnp.bfloat16)
    grad_g = lax.dot_general(rows, d_gate, (((0,), (0,)), ((), ())), preferred_element_type=jnp.float32).astype(jnp.bfloat16)
    grad_u = lax.dot_general(rows, d_upper, (((0,), (0,)), ((), ())), preferred_element_type=jnp.float32).astype(jnp.bfloat16)
    grad_d = lax.dot_general(hidden, cotangent, (((0,), (0,)), ((), ())), preferred_element_type=jnp.float32).astype(jnp.bfloat16)
    return output, d_rows, grad_g, grad_u, grad_d


def reference(tokens, expert_ids, combine, w_gate, w_up, w_down, grad_out):
    x_all = tokens.reshape(N_DP, N_EXPERT, TOK_DEV, D)
    id_all = expert_ids.reshape(N_DP, N_EXPERT, TOK_DEV, TOPK)
    c_all = combine.reshape(N_DP, N_EXPERT, TOK_DEV, TOPK)
    g_all = grad_out.reshape(N_DP, N_EXPERT, TOK_DEV, D)
    owners = jnp.arange(TOK_DEV * TOPK, dtype=jnp.int32) // TOPK

    def pack_source(x_dev, ids, c_dev, g_dev):
        flat, ranks = slot_table(ids)
        cot = (c_dev[:, :, None] * g_dev[:, None, :].astype(jnp.float32)).astype(jnp.bfloat16).reshape(TOK_DEV * TOPK, D)
        empty = jnp.zeros((EXPERTS, CAP, D), jnp.bfloat16)
        return empty.at[flat, ranks].set(x_dev[owners]), empty.at[flat, ranks].set(cot)

    def unpack_source(back, dback, ids, c_dev):
        flat, ranks = slot_table(ids)
        outs = back[flat, ranks].reshape(TOK_DEV, TOPK, D).astype(jnp.float32)
        drows = dback[flat, ranks].reshape(TOK_DEV, TOPK, D).astype(jnp.float32)
        mixed = jnp.sum(c_dev[:, :, None] * outs, axis=1).astype(jnp.bfloat16)
        return mixed, jnp.sum(drows, axis=1).astype(jnp.bfloat16)

    def one_expert(items):
        return expert_pass(*items)

    def one_row(totals, inputs):
        x_row, id_row, c_row, g_row = inputs
        sent_x, sent_c = jax.vmap(pack_source)(x_row, id_row, c_row, g_row)
        sent_x = jnp.swapaxes(sent_x, 0, 1).reshape(EXPERTS, N_EXPERT * CAP, D)
        sent_c = jnp.swapaxes(sent_c, 0, 1).reshape(EXPERTS, N_EXPERT * CAP, D)
        outs, drows, grad_g, grad_u, grad_d = lax.map(one_expert, (sent_x, sent_c, w_gate, w_up, w_down))
        outs = jnp.swapaxes(outs.reshape(EXPERTS, N_EXPERT, CAP, D), 0, 1)
        drows = jnp.swapaxes(drows.reshape(EXPERTS, N_EXPERT, CAP, D), 0, 1)
        mixed, grad_x = jax.vmap(unpack_source)(outs, drows, id_row, c_row)
        totals = (totals[0] + grad_g.astype(jnp.float32), totals[1] + grad_u.astype(jnp.float32), totals[2] + grad_d.astype(jnp.float32))
        return totals, (mixed, grad_x)

    start = (jnp.zeros((EXPERTS, D, H), jnp.float32), jnp.zeros((EXPERTS, D, H), jnp.float32), jnp.zeros((EXPERTS, H, D), jnp.float32))
    totals, (mixed, grad_x) = lax.scan(one_row, start, (x_all, id_all, c_all, g_all))
    return (mixed.reshape(TOKENS, D), grad_x.reshape(TOKENS, D), totals[0].astype(jnp.bfloat16), totals[1].astype(jnp.bfloat16), totals[2].astype(jnp.bfloat16))
```

```python
import functools

import jax
import jax.numpy as jnp
from jax import lax
from jax.experimental import pallas as pl
from jax.experimental.pallas import tpu as pltpu
from jax.sharding import PartitionSpec as P

BF = jnp.bfloat16
F32 = jnp.float32

NZ, NY = 8, 4
NX, NC = 4, 2
CAP = 16
LANES = NY * CAP
META = 128
CHUNKS = ((0, 1, -1, 2, -2, 3, -3, 4),)
VMEM_LIMIT = 56 * 1024 * 1024


def perm_z(k):
    return [(NY * z + y, NY * ((z + k) % NZ) + y) for z in range(NZ) for y in range(NY)]


def perm_y(k):
    return [(NY * z + y, NY * z + (y + k) % NY) for z in range(NZ) for y in range(NY)]


def perm_x(k):
    return [(NC * x + c, NC * ((x + k) % NX) + c) for x in range(NX) for c in range(NC)]


PERM_CORE = [(NC * x + c, NC * x + 1 - c) for x in range(NX) for c in range(NC)]


def along_z(value, k):
    return lax.ppermute(value, "expert", perm_z(k))


def along_y(value, k):
    return lax.ppermute(value, "expert", perm_y(k)) if k % NY else value


def whole(n=1):
    return [pl.BlockSpec(memory_space=pltpu.VMEM)] * n


def params(**kw):
    return pltpu.CompilerParams(vmem_limit_bytes=VMEM_LIMIT, **kw)


def cost(flops, nbytes):
    return pl.CostEstimate(flops=int(flops), bytes_accessed=int(nbytes), transcendentals=0)


def stacked(refs):
    return jnp.concatenate([r[...] for r in refs], axis=0)


def tn(a, b):
    return lax.dot_general(a, b, (((0,), (0,)), ((), ())), preferred_element_type=F32)


def nt(a, b):
    return lax.dot_general(a, b, (((1,), (1,)), ((), ())), preferred_element_type=F32)


def nn(a, b):
    return jnp.dot(a, b, preferred_element_type=F32)


def prep_kernel(x_ref, ids_ref, comb_ref, out_ref):
    tok, width = x_ref.shape
    top = ids_ref.shape[0]
    c = comb_ref[...]
    hi = c.astype(BF).astype(F32)
    rows = jnp.concatenate(
        [ids_ref[...].astype(F32), hi, c - hi, jnp.zeros((META - 3 * top, tok), F32)], axis=0
    )
    rows = jnp.concatenate([rows, jnp.zeros((META, META - tok), F32)], axis=1)
    out_ref[:, :width] = x_ref[...]
    out_ref[:, width:] = rows.T[:tok].astype(BF)


def prep(tokens, ids_t, comb_t):
    tok, width = tokens.shape
    return pl.pallas_call(
        prep_kernel,
        out_shape=jax.ShapeDtypeStruct((tok, width + META), BF),
        in_specs=whole(3),
        out_specs=whole()[0],
        compiler_params=params(),
    )(tokens, ids_t, comb_t)


def pack_x_kernel(n, top, lane_ref, *refs):
    xs, outs, (sel_ref, hi_ref, lo_ref) = refs[:n], refs[n : n + NY], refs[n + NY :]
    tok = xs[0].shape[0]
    width = xs[0].shape[1] - META
    lane_e = lane_ref[0:1, :LANES]
    slot = (lax.broadcasted_iota(jnp.int32, (tok, LANES), 1) % CAP).astype(F32)
    earlier = lax.broadcasted_iota(jnp.int32, (tok, tok), 0) > lax.broadcasted_iota(jnp.int32, (tok, tok), 1)
    earlier = jnp.where(earlier, 1.0, 0.0).astype(BF)
    for i in range(n):
        meta = xs[i][:, width:].astype(F32)
        chosen = jnp.zeros((tok, LANES), F32)
        hi = jnp.zeros((tok, LANES), F32)
        lo = jnp.zeros((tok, LANES), F32)
        for j in range(top):
            hit = meta[:, j : j + 1] == lane_e
            chosen += jnp.where(hit, 1.0, 0.0)
            hi += jnp.where(hit, meta[:, top + j : top + j + 1], 0.0)
            lo += jnp.where(hit, meta[:, 2 * top + j : 2 * top + j + 1], 0.0)
        rank = nn(earlier, chosen.astype(BF))
        here = rank == slot
        sel = jnp.where(here, chosen, 0.0).astype(BF)
        sel_ref[i] = sel
        hi_ref[i] = jnp.where(here, hi, 0.0).astype(BF)
        lo_ref[i] = jnp.where(here, lo, 0.0).astype(BF)
        rows = tn(sel, xs[i][:, :width]).astype(BF)
        for k in range(NY):
            outs[k][i * CAP : (i + 1) * CAP, :] = rows[k * CAP : (k + 1) * CAP]


def pack_x(lane_experts, blocks, top):
    n = len(blocks)
    tok, width = blocks[0].shape[0], blocks[0].shape[1] - META
    tables = jax.ShapeDtypeStruct((n, tok, LANES), BF)
    out = pl.pallas_call(
        functools.partial(pack_x_kernel, n, top),
        out_shape=[jax.ShapeDtypeStruct((n * CAP, width), BF)] * NY + [tables] * 3,
        in_specs=whole(1 + n),
        out_specs=whole(NY + 3),
        compiler_params=params(),
        cost_estimate=cost(2 * n * LANES * tok * width, 2 * n * (tok + LANES) * width),
    )(lane_experts, *blocks)
    return out[:NY], out[NY:]


def pack_g_kernel(n, *refs):
    gs, (hi_ref, lo_ref), outs = refs[:n], refs[n : n + 2], refs[n + 2 :]
    for i in range(n):
        rows = (tn(hi_ref[i], gs[i][...]) + tn(lo_ref[i], gs[i][...])).astype(BF)
        for k in range(NY):
            outs[k][i * CAP : (i + 1) * CAP, :] = rows[k * CAP : (k + 1) * CAP]


def pack_g(blocks, hi, lo):
    n = len(blocks)
    tok, width = blocks[0].shape
    return pl.pallas_call(
        functools.partial(pack_g_kernel, n),
        out_shape=[jax.ShapeDtypeStruct((n * CAP, width), BF)] * NY,
        in_specs=whole(n + 2),
        out_specs=whole(NY),
        compiler_params=params(),
        cost_estimate=cost(4 * n * LANES * tok * width, 2 * n * (tok + LANES) * width),
    )(*blocks, hi, lo)


def combine_kernel(jobs, *refs):
    refs = list(refs)
    ins = [([refs.pop(0) for _ in range(tables)], [refs.pop(0) for _ in range(NY)], [refs.pop(0) for _ in range(sums)]) for tables, sums in jobs]
    for (tables, rows, sums), out in zip(ins, refs):
        value = stacked(rows)
        total = nn(tables[0][...], value)
        for t in tables[1:]:
            total += nn(t[...], value)
        for s in sums:
            total += s[...].astype(F32)
        out[...] = total.astype(BF)


def combine(jobs):
    specs, args, outs, kinds = [], [], [], []
    for tables, rows, i, sums in jobs:
        tok, lanes = tables[0].shape[1:]
        width = rows[0].shape[1]
        specs += [pl.BlockSpec((None, tok, lanes), lambda _, i=i: (i, 0, 0))] * len(tables)
        specs += [pl.BlockSpec((CAP, width), lambda _, i=i: (i, 0))] * NY
        specs += [pl.BlockSpec((tok, width), lambda _: (0, 0))] * len(sums)
        args += [*tables, *rows, *sums]
        outs.append(jax.ShapeDtypeStruct((tok, width), BF))
        kinds.append((len(tables), len(sums)))
    return pl.pallas_call(
        functools.partial(combine_kernel, tuple(kinds)),
        grid=(1,),
        out_shape=outs,
        in_specs=specs,
        out_specs=[pl.BlockSpec(o.shape, lambda _: (0, 0)) for o in outs],
        compiler_params=params(),
        cost_estimate=cost(len(jobs) * 4 * outs[0].size * LANES, len(jobs) * 8 * outs[0].size),
    )(*args)


def spread(refs, value, cols=slice(None)):
    at = 0
    for r in refs:
        r[:, cols] = value[at : at + r.shape[0]]
        at += r.shape[0]


def fwd_kernel(nb, nh, *refs):
    xs, (wg, wu, wd) = refs[:nb], refs[nb : nb + 3]
    outs = refs[nb + 3 : 2 * nb + 3]
    hid_ref, a_ref, b_ref, hid = refs[2 * nb + 3 :]
    step = pl.program_id(0)

    @pl.when(step < nh)
    def _():
        x = stacked(xs)
        gate = nn(x, wg[...])
        upper = nn(x, wu[...])
        s = jax.nn.sigmoid(gate)
        silu = gate * s
        h = (silu * upper).astype(BF)
        a_ref[...] = upper * s * (1.0 + gate * (1.0 - s))
        b_ref[...] = silu
        hid_ref[...] = h
        hid[step] = h

    @pl.when(step >= nh)
    def _():
        h = jnp.concatenate([hid[i] for i in range(nh)], axis=1)
        spread(outs, nn(h, wd[...]).astype(BF))


def forward(xs, wg, wu, wd):
    nb = len(xs)
    _, width, hidden = wg.shape
    rows = sum(x.shape[0] for x in xs)
    th, tw = 256, 512
    nh, nw = hidden // th, width // tw
    first = lambda s: (0, 0, jnp.minimum(s, nh - 1))
    tile = lambda s: (0, jnp.minimum(s, nh - 1))
    second = lambda s: (0, jnp.maximum(s - nh, 0))
    out = pl.pallas_call(
        functools.partial(fwd_kernel, nb, nh),
        grid=(nh + nw,),
        out_shape=[jax.ShapeDtypeStruct(x.shape, BF) for x in xs]
        + [jax.ShapeDtypeStruct((rows, hidden), BF)]
        + [jax.ShapeDtypeStruct((rows, hidden), F32)] * 2,
        in_specs=[pl.BlockSpec(x.shape, lambda s: (0, 0)) for x in xs]
        + [pl.BlockSpec((None, width, th), first)] * 2
        + [pl.BlockSpec((None, hidden, tw), lambda s: (0, 0, jnp.maximum(s - nh, 0)))],
        out_specs=[pl.BlockSpec((x.shape[0], tw), second) for x in xs] + [pl.BlockSpec((rows, th), tile)] * 3,
        scratch_shapes=[pltpu.VMEM((nh, rows, th), BF)],
        compiler_params=params(),
        cost_estimate=cost(6 * rows * width * hidden, 6 * width * hidden + 4 * rows * width + 10 * rows * hidden),
    )(*xs, wg, wu, wd)
    return out[:nb], out[nb], out[nb + 1], out[nb + 2]


def bwd_kernel(nb, nh, *refs):
    cs, (a_ref, b_ref, wd, wg, wu) = refs[:nb], refs[nb : nb + 5]
    outs = refs[nb + 5 : 2 * nb + 5]
    dg_ref, du_ref, dg, du = refs[2 * nb + 5 :]
    step = pl.program_id(0)

    @pl.when(step < nh)
    def _():
        d_hidden = nt(stacked(cs), wd[...])
        g = (d_hidden * a_ref[...]).astype(BF)
        u = (d_hidden * b_ref[...]).astype(BF)
        dg_ref[...] = g
        du_ref[...] = u
        dg[step] = g
        du[step] = u

    @pl.when(step >= nh)
    def _():
        g = jnp.concatenate([dg[i] for i in range(nh)], axis=1)
        u = jnp.concatenate([du[i] for i in range(nh)], axis=1)
        spread(outs, (nt(g, wg[...]) + nt(u, wu[...])).astype(BF))


def backward(cs, a, b, wg, wu, wd):
    nb = len(cs)
    _, width, hidden = wg.shape
    rows = sum(x.shape[0] for x in cs)
    th, tw = 256, 512
    nh, nw = hidden // th, width // tw
    tile = lambda s: (0, jnp.minimum(s, nh - 1))
    second = lambda s: (0, jnp.maximum(s - nh, 0))
    out = pl.pallas_call(
        functools.partial(bwd_kernel, nb, nh),
        grid=(nh + nw,),
        out_shape=[jax.ShapeDtypeStruct(x.shape, BF) for x in cs] + [jax.ShapeDtypeStruct((rows, hidden), BF)] * 2,
        in_specs=[pl.BlockSpec(x.shape, lambda s: (0, 0)) for x in cs]
        + [pl.BlockSpec((rows, th), tile)] * 2
        + [pl.BlockSpec((None, th, width), lambda s: (0, jnp.minimum(s, nh - 1), 0))]
        + [pl.BlockSpec((None, tw, hidden), lambda s: (0, jnp.maximum(s - nh, 0), 0))] * 2,
        out_specs=[pl.BlockSpec((x.shape[0], tw), second) for x in cs] + [pl.BlockSpec((rows, th), tile)] * 2,
        scratch_shapes=[pltpu.VMEM((nh, rows, th), BF)] * 2,
        compiler_params=params(),
        cost_estimate=cost(6 * rows * width * hidden, 6 * width * hidden + 4 * rows * width + 12 * rows * hidden),
    )(*cs, a, b, wd, wg, wu)
    return out[:nb], out[nb], out[nb + 1]


def grad_kernel(nb, nd, sums, flip, _, *refs):
    refs = list(refs)
    rows = stacked([refs.pop(0) for _ in range(nb)])
    ds = [refs.pop(0) for _ in range(nd)]
    adds = [refs.pop(0) for _ in range(sums)]
    for i, d in enumerate(ds):
        value = tn(d[...], rows) if flip else tn(rows, d[...])
        if sums:
            value += adds[0][i].astype(F32)
        value = value.astype(BF)
        for j, out in enumerate(refs):
            if len(refs) == 1:
                out[i] = value
            else:

                @pl.when(pl.program_id(0) == j)
                def _(out=out, i=i, value=value):
                    out[i] = value


def grads(order, blocks, ds, received, flip):
    nb, nd = len(blocks), len(ds)
    width = blocks[0].shape[1]
    rows, hidden = ds[0].shape
    step = width // (NX * NC)
    shape = (hidden, step) if flip else (step, hidden)
    block = (None, nd, *shape)
    if received is None:
        out_shape = [jax.ShapeDtypeStruct((NX, nd, *shape), BF)]
        out_specs = [pl.BlockSpec(block, lambda j, o: (j, 0, 0, 0))]
    else:
        out_shape = [jax.ShapeDtypeStruct((nd, *shape), BF)] * NX
        out_specs = [pl.BlockSpec((nd, *shape), lambda j, o: (0, 0, 0))] * NX
    adds = [] if received is None else [received]
    return pl.pallas_call(
        functools.partial(grad_kernel, nb, nd, len(adds), flip),
        out_shape=out_shape,
        grid_spec=pltpu.PrefetchScalarGridSpec(
            num_scalar_prefetch=1,
            grid=(NX,),
            in_specs=[pl.BlockSpec((b.shape[0], step), lambda j, o: (0, o[j])) for b in blocks]
            + [pl.BlockSpec((rows, hidden), lambda j, o: (0, 0))] * nd
            + [pl.BlockSpec(block, lambda j, o: (j, 0, 0, 0))] * len(adds),
            out_specs=out_specs,
        ),
        compiler_params=params(),
        cost_estimate=cost(nd * rows * width * hidden, 2 * rows * (nd * hidden + width // 2) + 4 * nd * hidden * width),
    )(order, *blocks, *ds, *adds)


def reduced(order, order_other, blocks, ds, flip):
    to_other = grads(order_other, blocks, ds, None, flip)[0]
    received = lax.ppermute(to_other, "dp", PERM_CORE)
    own = grads(order, blocks, ds, received, flip)
    arrived = [own[0]] + [lax.ppermute(own[j], "dp", perm_x(j)) for j in range(1, NX)]
    total = arrived[0].astype(F32)
    for a in arrived[1:]:
        total = total + a.astype(F32)
    return total.astype(BF)


def gather_z(own, last):
    blocks = {0: own}
    up = down = own
    for r in range(1, NZ // 2):
        up, down = along_z(up, 1), along_z(down, -1)
        blocks[-r], blocks[r] = up, down
    blocks[NZ // 2] = along_z(up, 1) if last > 0 else along_z(down, -1)
    return blocks


def scatter_z(job, last):
    far, near = (1, -1) if last > 0 else (-1, 1)
    half = NZ // 2
    long, short = combine([job(half, []), job(-far * (half - 1), [])])
    long, short = along_z(long, far), along_z(short, near)
    for r in range(half - 1, 1, -1):
        long, short = combine([job(far * r, [long]), job(-far * (r - 1), [short])])
        long, short = along_z(long, far), along_z(short, near)
    (long,) = combine([job(far, [long])])
    long = along_z(long, far)
    return combine([job(0, [long, short])])[0]


def on_device(tokens, expert_ids, combine_w, w_gate, w_up, w_down, grad_out):
    top = expert_ids.shape[1]
    me = lax.axis_index("expert")
    z, y = me // NY, me % NY
    k = jnp.arange(META, dtype=jnp.int32) // CAP
    lane_experts = jnp.broadcast_to((z * NY + (y + k) % NY).astype(F32), (8, META))
    me_dp = lax.axis_index("dp")
    x, c = me_dp // NC, me_dp % NC
    j = jnp.arange(NX, dtype=jnp.int32)
    order = NC * ((x + j) % NX) + c
    order_other = NC * ((x + j) % NX) + (1 - c)

    with jax.named_scope("dispatch_tokens"):
        x_blocks = gather_z(prep(tokens, expert_ids.T, combine_w.T), 1)
    with jax.named_scope("dispatch_grads"):
        g_blocks = gather_z(grad_out, -1)

    where = {off: (n, i) for n, chunk in enumerate(CHUNKS) for i, off in enumerate(chunk)}
    x_rows, c_rows, tables = [], [], []
    for chunk in CHUNKS:
        packed, t = pack_x(lane_experts, [x_blocks[o] for o in chunk], top)
        tables.append(t)
        x_rows += [along_y(packed[k], k) for k in range(NY)]
    for n, chunk in enumerate(CHUNKS):
        packed = pack_g([g_blocks[o] for o in chunk], tables[n][1], tables[n][2])
        c_rows += [along_y(packed[k], k) for k in range(NY)]

    with jax.named_scope("expert"):
        out_rows, hid, a, b = forward(x_rows, w_gate, w_up, w_down)
    with jax.named_scope("return_out"):
        back = [along_y(o, -(i % NY)) for i, o in enumerate(out_rows)]
    with jax.named_scope("expert"):
        d_rows, dg, du = backward(c_rows, a, b, w_gate, w_up, w_down)
    with jax.named_scope("return_rows"):
        d_back = [along_y(o, -(i % NY)) for i, o in enumerate(d_rows)]

    with jax.named_scope("weight_grads"):
        grad_down = reduced(order, order_other, c_rows, [hid], True)
        grad_in = reduced(order, order_other, x_rows, [dg, du], False)

    def job(rows, picked):
        def part(off, sums):
            n, i = where[off]
            return ([tables[n][p] for p in picked], rows[n * NY : (n + 1) * NY], i, sums)

        return part

    with jax.named_scope("return_out"):
        mixed = scatter_z(job(back, (1, 2)), 1)
    with jax.named_scope("return_rows"):
        grad_tokens = scatter_z(job(d_back, (0,)), -1)
    return (mixed, grad_tokens, grad_in[0][None], grad_in[1][None], grad_down)


def solution(mesh):
    tok = P(("dp", "expert"), None)
    weight = P("expert", None, None)
    return jax.shard_map(
        on_device,
        mesh=mesh,
        in_specs=(tok, tok, tok, weight, weight, weight, tok),
        out_specs=(tok, tok, P("expert", "dp", None), P("expert", "dp", None), P("expert", None, "dp")),
        check_vma=False,
    )
```

```python
import functools

import jax
import jax.numpy as jnp
from jax import lax
from jax.experimental import pallas as pl
from jax.experimental.pallas import tpu as pltpu
from jax.sharding import PartitionSpec as P

BF = jnp.bfloat16
F32 = jnp.float32

NZ, NY = 8, 4
NX, NC = 4, 2
CAP = 16
LANES = NY * CAP
META = 128
CHUNKS = ((0, 1, -1, 2), (-2, 3, -3, 4))
BACK = ((1, (4, -3)), (1, (3, -2)), (0, (2, -1)), (0, (1, 0)))
VMEM_LIMIT = 12 * 1024 * 1024


def perm_z(k):
    return [(NY * z + y, NY * ((z + k) % NZ) + y) for z in range(NZ) for y in range(NY)]


def perm_y(k):
    return [(NY * z + y, NY * z + (y + k) % NY) for z in range(NZ) for y in range(NY)]


def perm_x(k):
    return [(NC * x + c, NC * ((x + k) % NX) + c) for x in range(NX) for c in range(NC)]


GROUPS_X = [[NC * x + c for x in range(NX)] for c in range(NC)]
PERM_CORE = [(NC * x + c, NC * x + 1 - c) for x in range(NX) for c in range(NC)]


def along_z(value, k):
    return lax.ppermute(value, "expert", perm_z(k))


def along_y(value, k):
    return lax.ppermute(value, "expert", perm_y(k)) if k % NY else value


def whole(n=1):
    return [pl.BlockSpec(memory_space=pltpu.VMEM)] * n


def params(limit=VMEM_LIMIT):
    return pltpu.CompilerParams(vmem_limit_bytes=limit)


TINY = pl.CostEstimate(flops=1, bytes_accessed=1, transcendentals=0)
LONG = pl.CostEstimate(flops=20000000000, bytes_accessed=1, transcendentals=0)


def unread(n):
    return [pl.BlockSpec(memory_space=pl.ANY)] * n


def bf16(*shape):
    return jax.ShapeDtypeStruct(shape, BF)


MARK = jax.ShapeDtypeStruct((8, 128), F32)


def tn(a, b):
    return lax.dot_general(a, b, (((0,), (0,)), ((), ())), preferred_element_type=F32)


def nt(a, b):
    return lax.dot_general(a, b, (((1,), (1,)), ((), ())), preferred_element_type=F32)


def nn(a, b):
    return jnp.dot(a, b, preferred_element_type=F32)


def prep_kernel(x_ref, g_ref, ids_ref, comb_ref, out_ref):
    tok, width = x_ref.shape
    top = ids_ref.shape[0]
    c = comb_ref[...]
    hi = c.astype(BF).astype(F32)
    rows = jnp.concatenate(
        [ids_ref[...].astype(F32), hi, c - hi, jnp.zeros((META - 3 * top, tok), F32)], axis=0
    )
    rows = jnp.concatenate([rows, jnp.zeros((META, META - tok), F32)], axis=1)
    out_ref[:, :width] = x_ref[...]
    out_ref[:, width : width + META] = rows.T[:tok].astype(BF)
    out_ref[:, width + META :] = g_ref[...]


def prep(tokens, grad_out, ids_t, comb_t):
    tok, width = tokens.shape
    args = (tokens, grad_out, ids_t, comb_t)
    return pl.pallas_call(
        prep_kernel,
        grid=(1,),
        out_shape=bf16(tok, 2 * width + META),
        in_specs=[pl.BlockSpec(a.shape, lambda i: (0, 0)) for a in args],
        out_specs=pl.BlockSpec((tok, 2 * width + META), lambda i: (0, 0)),
        compiler_params=params(60 * 1024 * 1024),
        cost_estimate=TINY,
        name="prep",
    )(*args)


def halves_kernel(up, down, x_ref, g_ref):
    width = x_ref.shape[1]
    x_ref[...] = up[:, :width]
    g_ref[...] = down[:, width:]


def halves(up, down, width):
    tok, full = up.shape
    return pl.pallas_call(
        halves_kernel,
        out_shape=[bf16(tok, width), bf16(tok, full - width)],
        in_specs=whole(2),
        out_specs=whole(2),
        compiler_params=params(),
        cost_estimate=TINY,
        name="halves",
    )(up, down)


def pack_kernel(arity, top, later, *refs):
    refs = list(refs)
    sources = [[refs.pop(0) for _ in range(a)] for a in arity]
    refs = refs[later:]
    outs, (sel_ref, mix_ref) = refs[:NY], refs[NY:]
    tok = sources[0][0].shape[0]
    width = (outs[0].shape[1]) // 2
    me = lax.axis_index("expert")
    lane_y = (me % NY + lax.broadcasted_iota(jnp.int32, (1, LANES), 1) // CAP) % NY
    lane_e = (me - me % NY + lane_y).astype(F32)
    slot = (lax.broadcasted_iota(jnp.int32, (tok, LANES), 1) % CAP).astype(F32)
    earlier = lax.broadcasted_iota(jnp.int32, (tok, tok), 0) > lax.broadcasted_iota(jnp.int32, (tok, tok), 1)
    earlier = jnp.where(earlier, 1.0, 0.0).astype(BF)
    for i, refs_i in enumerate(sources):
        x_ref = refs_i[0]
        g = refs_i[1][...] if len(refs_i) > 1 else x_ref[:, width + META :]
        meta = x_ref[:, width : width + META].astype(F32)
        chosen = jnp.zeros((tok, LANES), F32)
        hi = jnp.zeros((tok, LANES), F32)
        lo = jnp.zeros((tok, LANES), F32)
        for j in range(top):
            hit = meta[:, j : j + 1] == lane_e
            chosen = jnp.where(hit, 1.0, chosen)
            hi = jnp.where(hit, meta[:, top + j : top + j + 1], hi)
            lo = jnp.where(hit, meta[:, 2 * top + j : 2 * top + j + 1], lo)
        here = nn(earlier, chosen.astype(BF)) == slot
        sel = jnp.where(here, chosen, 0.0).astype(BF)
        hi = jnp.where(here, hi, 0.0).astype(BF)
        lo = jnp.where(here, lo, 0.0).astype(BF)
        sel_ref[i] = sel
        mix_ref[i] = jnp.concatenate([hi, lo], axis=1)
        rows = tn(sel, x_ref[:, :width]).astype(BF)
        cots = (tn(hi, g) + tn(lo, g)).astype(BF)
        for k in range(NY):
            outs[k][i * CAP : (i + 1) * CAP, :width] = rows[k * CAP : (k + 1) * CAP]
            outs[k][i * CAP : (i + 1) * CAP, width:] = cots[k * CAP : (k + 1) * CAP]


def pack(blocks, top, width, cost_estimate, after=()):
    n = len(blocks)
    tok = blocks[0][0].shape[0]
    flat = [a for b in blocks for a in b]
    out = pl.pallas_call(
        functools.partial(pack_kernel, tuple(len(b) for b in blocks), top, len(after)),
        out_shape=[jax.ShapeDtypeStruct((n * CAP, 2 * width), BF)] * NY
        + [jax.ShapeDtypeStruct((n, tok, LANES), BF), jax.ShapeDtypeStruct((n, tok, 2 * LANES), BF)],
        in_specs=whole(len(flat)) + unread(len(after)),
        out_specs=whole(NY + 2),
        compiler_params=params(),
        cost_estimate=cost_estimate,
        name="pack",
    )(*flat, *after)
    return out[:NY], out[NY:]


def unpack_kernel(picked, split, later, sel_ref, mix_ref, *refs):
    rows, outs = refs[:NY], list(refs[NY + later :])
    width = rows[0].shape[1] // 2
    for n, i in enumerate(picked):
        mine = jnp.concatenate([r[n * CAP : (n + 1) * CAP] for r in rows], axis=0)
        out, d_row = mine[:, :width], mine[:, width:]
        mixed = nn(mix_ref[i], jnp.concatenate([out, out], axis=0)).astype(BF)
        toks = nn(sel_ref[i], d_row).astype(BF)
        if n in split:
            outs.pop(0)[...] = mixed
            outs.pop(0)[...] = toks
        else:
            ref = outs.pop(0)
            ref[:, :width] = mixed
            ref[:, width:] = toks


def unpack(tables, picked, rows, split, after=()):
    sel, mix = tables
    tok, width = sel.shape[1], rows[0].shape[1] // 2
    shapes = []
    for n in range(len(picked)):
        shapes += [bf16(tok, width)] * 2 if n in split else [bf16(tok, 2 * width)]
    out = pl.pallas_call(
        functools.partial(unpack_kernel, picked, split, len(after)),
        out_shape=shapes,
        in_specs=whole(2 + NY) + unread(len(after)),
        out_specs=whole(len(shapes)),
        compiler_params=params(),
        cost_estimate=TINY,
        name="unpack",
    )(sel, mix, *rows, *after)
    out = list(out)
    return [(out.pop(0), out.pop(0)) if n in split else (out.pop(0),) for n in range(len(picked))]


def add_kernel(jobs, later, *refs):
    refs = list(refs)
    ins = [(refs.pop(0), [refs.pop(0) for _ in offs]) for offs in jobs]
    refs = refs[later:]
    step = 256
    for (base, adds), offs, out in zip(ins, jobs, refs):
        for at in range(0, base.shape[1], step):
            total = base[:, at : at + step].astype(F32)
            for a, off in zip(adds, offs):
                if off <= at < off + a.shape[1]:
                    total = total + a[:, at - off : at - off + step].astype(F32)
            out[:, at : at + step] = total.astype(BF)


def add(jobs, cost_estimate, after=()):
    args, offs = [], []
    for base, adds in jobs:
        args += [base, *[a for a, _ in adds]]
        offs.append(tuple(o for _, o in adds))
    return pl.pallas_call(
        functools.partial(add_kernel, tuple(offs), len(after)),
        out_shape=[bf16(*b.shape) for b, _ in jobs],
        in_specs=whole(len(args)) + unread(len(after)),
        out_specs=whole(len(jobs)),
        compiler_params=params(),
        cost_estimate=cost_estimate,
        name="add",
    )(*args, *after)


def last_kernel(base, up, down, mark, mixed, toks):
    width = mixed.shape[1]
    total = base[...].astype(F32) + up[...].astype(F32) + down[...].astype(F32)
    mixed[...] = total[:, :width].astype(BF)
    toks[...] = total[:, width:].astype(BF)


def last(base, up, down, mark):
    tok, width = base.shape
    return pl.pallas_call(
        last_kernel,
        out_shape=[bf16(tok, width // 2)] * 2,
        in_specs=whole(3) + unread(1),
        out_specs=whole(2),
        compiler_params=params(),
        cost_estimate=TINY,
        name="last",
    )(base, up, down, mark)


def hidden_kernel(nb, later, *refs):
    xs, (wg, wu, wd) = refs[:nb], refs[nb : nb + 3]
    hid_ref, dg_ref, du_ref, rows = refs[nb + 3 + later :]
    at = 0
    for r in xs:
        rows[at : at + r.shape[0]] = r[...]
        at += r.shape[0]
    _, width, hidden = wg.shape
    tile = 256
    for h in range(0, hidden, tile):
        cols = slice(h, h + tile)
        x = rows[:, :width]
        gate = nn(x, wg[0, :, cols])
        upper = nn(x, wu[0, :, cols])
        d_hidden = nt(rows[:, width:], wd[0, cols, :])
        s = jax.nn.sigmoid(gate)
        silu = gate * s
        hid_ref[:, cols] = (silu * upper).astype(BF)
        dg_ref[:, cols] = (d_hidden * upper * s * (1.0 + gate * (1.0 - s))).astype(BF)
        du_ref[:, cols] = (d_hidden * silu).astype(BF)


def hidden_of(xs, wg, wu, wd, after=()):
    rows = sum(x.shape[0] for x in xs)
    hidden = wg.shape[2]
    return pl.pallas_call(
        functools.partial(hidden_kernel, len(xs), len(after)),
        out_shape=[jax.ShapeDtypeStruct((rows, hidden), BF)] * 3 + [jax.ShapeDtypeStruct((rows, xs[0].shape[1]), BF)],
        in_specs=whole(len(xs) + 3) + unread(len(after)),
        out_specs=whole(4),
        compiler_params=params(),
        cost_estimate=TINY,
        name="hidden",
    )(*xs, wg, wu, wd, *after)


def rows_kernel(places, hid, dg, du, wg, wu, wd, *outs):
    outs[-1][...] = jnp.zeros_like(outs[-1])
    _, width, hidden = wg.shape
    tile = 512
    for n in range(0, width, tile):
        cols = slice(n, n + tile)
        out = nn(hid[...], wd[0, :, cols]).astype(BF)
        d_row = (nt(dg[...], wg[0, cols, :]) + nt(du[...], wu[0, cols, :])).astype(BF)
        for r, at in zip(outs, places):
            for i, p in enumerate(at):
                r[i * CAP : (i + 1) * CAP, cols] = out[p * CAP : (p + 1) * CAP]
                r[i * CAP : (i + 1) * CAP, width + n : width + n + tile] = d_row[p * CAP : (p + 1) * CAP]


def rows_of(places, hid, dg, du, wg, wu, wd):
    width = wg.shape[1]
    out = [bf16(len(at) * CAP, 2 * width) for at in places]
    return pl.pallas_call(
        functools.partial(rows_kernel, places),
        grid=(1,),
        out_shape=out + [MARK],
        in_specs=whole(6),
        out_specs=[pl.BlockSpec(o.shape, lambda i: (0, 0)) for o in out] + whole(),
        compiler_params=params(),
        cost_estimate=TINY,
        name="rows",
    )(hid, dg, du, wg, wu, wd)


def grad_kernel(nc, has_add, later, other, *refs):
    refs = list(refs)
    rows = [refs.pop(0) for _ in range(nc)]
    hid, dg, du = ([refs.pop(0) for _ in range(nc)] for _ in range(3))
    add = refs.pop(0) if has_add else None
    out, mark = refs[later:]
    width = rows[0].shape[1] // 2
    step = out.shape[1] // 3
    at = (NC * pl.program_id(0) + (lax.axis_index("dp") + other) % NC) * step

    def joined(refs, first=None):
        cols = slice(None) if first is None else pl.ds(pl.multiple_of(first, step), step)
        return jnp.concatenate([r[:, cols] for r in refs], axis=0)

    x, c = joined(rows, at), joined(rows, width + at)
    for i, (a, d) in enumerate(((x, dg), (x, du), (c, hid))):
        value = tn(a, joined(d))
        part = slice(i * step, (i + 1) * step)
        if has_add:
            value = value + add[pl.program_id(0), part, :].astype(F32)
        out[0, part, :] = value.astype(BF)
    mark[...] = jnp.zeros_like(mark)


def grads(other, rows, hids, received, after=()):
    hidden = hids[0][0].shape[1]
    step = rows[0].shape[1] // (2 * NX * NC)
    flat = [h[i] for i in range(3) for h in hids]
    return pl.pallas_call(
        functools.partial(grad_kernel, len(rows), bool(received), len(after), other),
        grid=(NX,),
        out_shape=[bf16(NX, 3 * step, hidden), MARK],
        in_specs=whole(len(rows) + len(flat) + len(received)) + unread(len(after)),
        out_specs=[pl.BlockSpec((1, 3 * step, hidden), lambda j: (j, 0, 0))] + whole(),
        compiler_params=params(),
        cost_estimate=TINY,
        name="grads",
    )(*rows, *flat, *received, *after)


def sum_kernel(arrived, gate, up, down, mark):
    step = gate.shape[0]

    def total(part):
        return sum(arrived[j, part * step : (part + 1) * step].astype(F32) for j in range(NX))

    gate[...] = total(0).astype(BF)
    up[...] = total(1).astype(BF)
    down[...] = total(2).T.astype(BF)
    mark[...] = jnp.zeros_like(mark)


def sums(arrived):
    _, rows, hidden = arrived.shape
    step = rows // 3
    return pl.pallas_call(
        sum_kernel,
        out_shape=[bf16(step, hidden)] * 2 + [bf16(hidden, step), MARK],
        in_specs=whole(),
        out_specs=whole(4),
        compiler_params=params(),
        cost_estimate=TINY,
        name="sums",
    )(arrived)


def on_device(tokens, expert_ids, combine_w, w_gate, w_up, w_down, grad_out):
    top, width = expert_ids.shape[1], tokens.shape[1]
    own = prep(tokens, grad_out, expert_ids.T, combine_w.T)
    blocks = {0: (own,)}
    up = down = own
    for r in range(1, NZ // 2):
        up, down = along_z(up, 1), along_z(down, -1)
        blocks[-r], blocks[r] = (up,), (down,)
    up, down = halves(up, down, width + META)
    blocks[NZ // 2] = (along_z(up, 1), along_z(down, -1))

    weights = (w_gate, w_up, w_down)
    tables, hids, all_rows, back = [], [], [], {}
    done = []
    for n, chunk in enumerate(CHUNKS):
        p, t = pack([blocks[o] for o in chunk], top, width, TINY)
        tables.append(t)
        *h, r = hidden_of([along_y(p[k], k) for k in range(NY)], *weights, done)
        hids.append(h)
        all_rows.append(r)
        mine = [offs for m, offs in BACK if m == n]
        places = [tuple(k * len(chunk) + chunk.index(o) for o in offs) for offs in mine for k in range(NY)]
        out = rows_of(tuple(places), *h, *weights)
        done = [out[-1]]
        for i, offs in enumerate(mine):
            back[offs] = [along_y(out[i * NY + k], -k) for k in range(NY)]

    def returned(n, after=()):
        chunk, offs = BACK[n]
        picked = tuple(CHUNKS[chunk].index(o) for o in offs)
        split = (offs.index(half),) if half in offs else ()
        return zip(offs, unpack(tables[chunk], picked, back[offs], split, after))

    half = NZ // 2
    other, _ = grads(1, all_rows, hids, [], done)
    own_grads, grads_done = grads(0, all_rows, hids, [lax.ppermute(other, "dp", PERM_CORE)])
    grad_gate, grad_up, grad_down, mark = sums(
        lax.all_to_all(own_grads, "dp", split_axis=0, concat_axis=0, tiled=True, axis_index_groups=GROUPS_X)
    )
    parts = dict(returned(0, [grads_done]))
    parts.update(returned(1))
    parts.update(returned(2))
    parts.update(returned(3))
    far_mixed, far_toks = parts[half]
    up, down = along_z(far_mixed, 1), along_z(far_toks, -1)
    up, down = add([(parts[half - 1][0], [(up, 0)]), (parts[1 - half][0], [(down, width)])], LONG)
    for r in range(half - 2, 0, -1):
        up, down = along_z(up, 1), along_z(down, -1)
        up, down = add([(parts[r][0], [(up, 0)]), (parts[-r][0], [(down, 0)])], TINY)
    up, down = along_z(up, 1), along_z(down, -1)
    mixed, grad_tokens = last(parts[0][0], up, down, mark)
    return (mixed, grad_tokens, grad_gate[None], grad_up[None], grad_down[None])


def solution(mesh):
    tok = P(("dp", "expert"), None)
    weight = P("expert", None, None)
    return jax.shard_map(
        on_device,
        mesh=mesh,
        in_specs=(tok, tok, tok, weight, weight, weight, tok),
        out_specs=(tok, tok, P("expert", "dp", None), P("expert", "dp", None), P("expert", None, "dp")),
        check_vma=False,
    )
```

```python
import functools

import jax
import jax.numpy as jnp
from jax import lax
from jax.experimental import pallas as pl
from jax.experimental.pallas import tpu as pltpu
from jax.sharding import PartitionSpec as P

BF = jnp.bfloat16
F32 = jnp.float32

NZ, NY = 8, 4
NX, NC = 4, 2
CAP = 16
LANES = NY * CAP
META = 128
CHUNKS = ((0, 1, -1, 2, -2), (3, -3, 4))
BACK = ((1, (4, 3, -3)), (0, (2, -2)), (0, (1, -1, 0)))
VMEM_LIMIT = 12 * 1024 * 1024


def perm_z(k):
    return [(NY * z + y, NY * ((z + k) % NZ) + y) for z in range(NZ) for y in range(NY)]


def perm_y(k):
    return [(NY * z + y, NY * z + (y + k) % NY) for z in range(NZ) for y in range(NY)]


def perm_x(k):
    return [(NC * x + c, NC * ((x + k) % NX) + c) for x in range(NX) for c in range(NC)]


GROUPS_X = [[NC * x + c for x in range(NX)] for c in range(NC)]
PERM_CORE = [(NC * x + c, NC * x + 1 - c) for x in range(NX) for c in range(NC)]


def along_z(value, k):
    return lax.ppermute(value, "expert", perm_z(k))


def along_y(value, k):
    return lax.ppermute(value, "expert", perm_y(k)) if k % NY else value


def whole(n=1):
    return [pl.BlockSpec(memory_space=pltpu.VMEM)] * n


def params(limit=VMEM_LIMIT):
    return pltpu.CompilerParams(vmem_limit_bytes=limit)


SHORT = pl.CostEstimate(flops=3000000000, bytes_accessed=1, transcendentals=0)
TINY = pl.CostEstimate(flops=1, bytes_accessed=1, transcendentals=0)
LONG = pl.CostEstimate(flops=20000000000, bytes_accessed=1, transcendentals=0)


def unread(n):
    return [pl.BlockSpec(memory_space=pl.ANY)] * n


def bf16(*shape):
    return jax.ShapeDtypeStruct(shape, BF)


MARK = jax.ShapeDtypeStruct((8, 128), F32)


def tn(a, b):
    return lax.dot_general(a, b, (((0,), (0,)), ((), ())), preferred_element_type=F32)


def nt(a, b):
    return lax.dot_general(a, b, (((1,), (1,)), ((), ())), preferred_element_type=F32)


def nn(a, b):
    return jnp.dot(a, b, preferred_element_type=F32)


def prep_kernel(x_ref, g_ref, ids_ref, comb_ref, out_ref):
    tok, width = x_ref.shape
    top = ids_ref.shape[0]
    c = comb_ref[...]
    hi = c.astype(BF).astype(F32)
    rows = jnp.concatenate(
        [ids_ref[...].astype(F32), hi, c - hi, jnp.zeros((META - 3 * top, tok), F32)], axis=0
    )
    rows = jnp.concatenate([rows, jnp.zeros((META, META - tok), F32)], axis=1)
    out_ref[:, :width] = x_ref[...]
    out_ref[:, width : width + META] = rows.T[:tok].astype(BF)
    out_ref[:, width + META :] = g_ref[...]


def prep(tokens, grad_out, ids_t, comb_t):
    tok, width = tokens.shape
    args = (tokens, grad_out, ids_t, comb_t)
    return pl.pallas_call(
        prep_kernel,
        grid=(1,),
        out_shape=bf16(tok, 2 * width + META),
        in_specs=[pl.BlockSpec(a.shape, lambda i: (0, 0)) for a in args],
        out_specs=pl.BlockSpec((tok, 2 * width + META), lambda i: (0, 0)),
        compiler_params=params(60 * 1024 * 1024),
        cost_estimate=TINY,
        name="prep",
    )(*args)


def halves_kernel(up, down, *refs):
    x_ref, g_ref = refs[-2:]
    width = x_ref.shape[1]
    x_ref[...] = up[:, :width]
    g_ref[...] = down[:, width:]


def halves(up, down, width, after):
    tok, full = up.shape
    return pl.pallas_call(
        halves_kernel,
        out_shape=[bf16(tok, width), bf16(tok, full - width)],
        in_specs=whole(2) + unread(len(after)),
        out_specs=whole(2),
        compiler_params=params(),
        cost_estimate=TINY,
        name="halves",
    )(up, down, *after)


def pack_kernel(arity, top, later, *refs):
    refs = list(refs)
    sources = [[refs.pop(0) for _ in range(a)] for a in arity]
    refs = refs[later:]
    outs, (sel_ref, mix_ref) = refs[:NY], refs[NY:]
    tok = sources[0][0].shape[0]
    width = (outs[0].shape[1]) // 2
    me = lax.axis_index("expert")
    lane_y = (me % NY + lax.broadcasted_iota(jnp.int32, (1, LANES), 1) // CAP) % NY
    lane_e = (me - me % NY + lane_y).astype(F32)
    slot = (lax.broadcasted_iota(jnp.int32, (tok, LANES), 1) % CAP).astype(F32)
    earlier = lax.broadcasted_iota(jnp.int32, (tok, tok), 0) > lax.broadcasted_iota(jnp.int32, (tok, tok), 1)
    earlier = jnp.where(earlier, 1.0, 0.0).astype(BF)
    for i, refs_i in enumerate(sources):
        x_ref = refs_i[0]
        g = refs_i[1][...] if len(refs_i) > 1 else x_ref[:, width + META :]
        meta = x_ref[:, width : width + META].astype(F32)
        chosen = jnp.zeros((tok, LANES), F32)
        hi = jnp.zeros((tok, LANES), F32)
        lo = jnp.zeros((tok, LANES), F32)
        for j in range(top):
            hit = meta[:, j : j + 1] == lane_e
            chosen = jnp.where(hit, 1.0, chosen)
            hi = jnp.where(hit, meta[:, top + j : top + j + 1], hi)
            lo = jnp.where(hit, meta[:, 2 * top + j : 2 * top + j + 1], lo)
        here = nn(earlier, chosen.astype(BF)) == slot
        sel = jnp.where(here, chosen, 0.0).astype(BF)
        hi = jnp.where(here, hi, 0.0).astype(BF)
        lo = jnp.where(here, lo, 0.0).astype(BF)
        sel_ref[i] = sel
        mix_ref[i] = jnp.concatenate([hi, lo], axis=1)
        rows = tn(sel, x_ref[:, :width]).astype(BF)
        cots = (tn(hi, g) + tn(lo, g)).astype(BF)
        for k in range(NY):
            outs[k][i * CAP : (i + 1) * CAP, :width] = rows[k * CAP : (k + 1) * CAP]
            outs[k][i * CAP : (i + 1) * CAP, width:] = cots[k * CAP : (k + 1) * CAP]


def pack(blocks, top, width, cost_estimate, after=()):
    n = len(blocks)
    tok = blocks[0][0].shape[0]
    flat = [a for b in blocks for a in b]
    out = pl.pallas_call(
        functools.partial(pack_kernel, tuple(len(b) for b in blocks), top, len(after)),
        out_shape=[jax.ShapeDtypeStruct((n * CAP, 2 * width), BF)] * NY
        + [jax.ShapeDtypeStruct((n, tok, LANES), BF), jax.ShapeDtypeStruct((n, tok, 2 * LANES), BF)],
        in_specs=whole(len(flat)) + unread(len(after)),
        out_specs=whole(NY + 2),
        compiler_params=params(),
        cost_estimate=cost_estimate,
        name="pack",
    )(*flat, *after)
    return out[:NY], out[NY:]


def unpack_kernel(picked, split, later, sel_ref, mix_ref, *refs):
    rows, outs = refs[:NY], list(refs[NY + later :])
    width = rows[0].shape[1] // 2
    for n, i in enumerate(picked):
        mine = jnp.concatenate([r[n * CAP : (n + 1) * CAP] for r in rows], axis=0)
        out, d_row = mine[:, :width], mine[:, width:]
        mixed = nn(mix_ref[i], jnp.concatenate([out, out], axis=0)).astype(BF)
        toks = nn(sel_ref[i], d_row).astype(BF)
        if n in split:
            outs.pop(0)[...] = mixed
            outs.pop(0)[...] = toks
        else:
            ref = outs.pop(0)
            ref[:, :width] = mixed
            ref[:, width:] = toks


def unpack(tables, picked, rows, split, cost_estimate, after=()):
    sel, mix = tables
    tok, width = sel.shape[1], rows[0].shape[1] // 2
    shapes = []
    for n in range(len(picked)):
        shapes += [bf16(tok, width)] * 2 if n in split else [bf16(tok, 2 * width)]
    out = pl.pallas_call(
        functools.partial(unpack_kernel, picked, split, len(after)),
        out_shape=shapes,
        in_specs=whole(2 + NY) + unread(len(after)),
        out_specs=whole(len(shapes)),
        compiler_params=params(),
        cost_estimate=cost_estimate,
        name="unpack",
    )(sel, mix, *rows, *after)
    out = list(out)
    return [(out.pop(0), out.pop(0)) if n in split else (out.pop(0),) for n in range(len(picked))]


def add_kernel(jobs, later, *refs):
    refs = list(refs)
    ins = [(refs.pop(0), [refs.pop(0) for _ in offs]) for offs in jobs]
    refs = refs[later:]
    step = 256
    for (base, adds), offs, out in zip(ins, jobs, refs):
        for at in range(0, base.shape[1], step):
            total = base[:, at : at + step].astype(F32)
            for a, off in zip(adds, offs):
                if off <= at < off + a.shape[1]:
                    total = total + a[:, at - off : at - off + step].astype(F32)
            out[:, at : at + step] = total.astype(BF)


def add(jobs, cost_estimate, after=()):
    args, offs = [], []
    for base, adds in jobs:
        args += [base, *[a for a, _ in adds]]
        offs.append(tuple(o for _, o in adds))
    return pl.pallas_call(
        functools.partial(add_kernel, tuple(offs), len(after)),
        out_shape=[bf16(*b.shape) for b, _ in jobs],
        in_specs=whole(len(args)) + unread(len(after)),
        out_specs=whole(len(jobs)),
        compiler_params=params(),
        cost_estimate=cost_estimate,
        name="add",
    )(*args, *after)


def last_kernel(base, up, down, mark, mixed, toks):
    width = mixed.shape[1]
    total = base[...].astype(F32) + up[...].astype(F32) + down[...].astype(F32)
    mixed[...] = total[:, :width].astype(BF)
    toks[...] = total[:, width:].astype(BF)


def last(base, up, down, mark):
    tok, width = base.shape
    return pl.pallas_call(
        last_kernel,
        out_shape=[bf16(tok, width // 2)] * 2,
        in_specs=whole(3) + unread(1),
        out_specs=whole(2),
        compiler_params=params(),
        cost_estimate=TINY,
        name="last",
    )(base, up, down, mark)


def hidden_kernel(nb, later, *refs):
    xs, (wg, wu, wd) = refs[:nb], refs[nb : nb + 3]
    hid_ref, dg_ref, du_ref, rows = refs[nb + 3 + later :]
    at = 0
    for r in xs:
        rows[at : at + r.shape[0]] = r[...]
        at += r.shape[0]
    _, width, hidden = wg.shape
    tile = 256
    for h in range(0, hidden, tile):
        cols = slice(h, h + tile)
        x = rows[:, :width]
        gate = nn(x, wg[0, :, cols])
        upper = nn(x, wu[0, :, cols])
        d_hidden = nt(rows[:, width:], wd[0, cols, :])
        s = jax.nn.sigmoid(gate)
        silu = gate * s
        hid_ref[:, cols] = (silu * upper).astype(BF)
        dg_ref[:, cols] = (d_hidden * upper * s * (1.0 + gate * (1.0 - s))).astype(BF)
        du_ref[:, cols] = (d_hidden * silu).astype(BF)


def hidden_of(xs, wg, wu, wd, after=()):
    rows = sum(x.shape[0] for x in xs)
    hidden = wg.shape[2]
    return pl.pallas_call(
        functools.partial(hidden_kernel, len(xs), len(after)),
        out_shape=[jax.ShapeDtypeStruct((rows, hidden), BF)] * 3 + [jax.ShapeDtypeStruct((rows, xs[0].shape[1]), BF)],
        in_specs=whole(len(xs) + 3) + unread(len(after)),
        out_specs=whole(4),
        compiler_params=params(),
        cost_estimate=TINY,
        name="hidden",
    )(*xs, wg, wu, wd, *after)


def rows_kernel(places, later, hid, dg, du, wg, wu, wd, *outs):
    outs = outs[later:]
    outs[-1][...] = jnp.zeros_like(outs[-1])
    _, width, hidden = wg.shape
    tile = 512
    for n in range(0, width, tile):
        cols = slice(n, n + tile)
        out = nn(hid[...], wd[0, :, cols]).astype(BF)
        d_row = (nt(dg[...], wg[0, cols, :]) + nt(du[...], wu[0, cols, :])).astype(BF)
        for r, at in zip(outs, places):
            for i, p in enumerate(at):
                r[i * CAP : (i + 1) * CAP, cols] = out[p * CAP : (p + 1) * CAP]
                r[i * CAP : (i + 1) * CAP, width + n : width + n + tile] = d_row[p * CAP : (p + 1) * CAP]


def rows_of(places, hid, dg, du, wg, wu, wd, cost_estimate, after=()):
    width = wg.shape[1]
    out = [bf16(len(at) * CAP, 2 * width) for at in places]
    return pl.pallas_call(
        functools.partial(rows_kernel, places, len(after)),
        grid=(1,),
        out_shape=out + [MARK],
        in_specs=whole(6) + unread(len(after)),
        out_specs=[pl.BlockSpec(o.shape, lambda i: (0, 0)) for o in out] + whole(),
        compiler_params=params(),
        cost_estimate=cost_estimate,
        name="rows",
    )(hid, dg, du, wg, wu, wd, *after)


def grad_kernel(nc, na, later, other, *refs):
    refs = list(refs)
    rows = [refs.pop(0) for _ in range(nc)]
    hid, dg, du = ([refs.pop(0) for _ in range(nc)] for _ in range(3))
    adds = [refs.pop(0) for _ in range(na)]
    out, mark = refs[later:]
    width = rows[0].shape[1] // 2
    step = out.shape[1] // 3
    at = (NC * pl.program_id(0) + (lax.axis_index("dp") + other) % NC) * step

    def joined(refs, first=None):
        cols = slice(None) if first is None else pl.ds(pl.multiple_of(first, step), step)
        return jnp.concatenate([r[:, cols] for r in refs], axis=0)

    x, c = joined(rows, at), joined(rows, width + at)
    for i, (a, d) in enumerate(((x, dg), (x, du), (c, hid))):
        value = tn(a, joined(d))
        part = slice(i * step, (i + 1) * step)
        for add in adds:
            value = value + add[pl.program_id(0), part, :].astype(F32)
        out[0, part, :] = value.astype(BF)
    mark[...] = jnp.zeros_like(mark)


def grads(other, rows, hids, received, after=()):
    hidden = hids[0][0].shape[1]
    step = rows[0].shape[1] // (2 * NX * NC)
    flat = [h[i] for i in range(3) for h in hids]
    return pl.pallas_call(
        functools.partial(grad_kernel, len(rows), len(received), len(after), other),
        grid=(NX,),
        out_shape=[bf16(NX, 3 * step, hidden), MARK],
        in_specs=whole(len(rows) + len(flat) + len(received)) + unread(len(after)),
        out_specs=[pl.BlockSpec((1, 3 * step, hidden), lambda j: (j, 0, 0))] + whole(),
        compiler_params=params(),
        cost_estimate=TINY,
        name="grads",
    )(*rows, *flat, *received, *after)


def sum_kernel(arrived, gate, up, down, mark):
    step = gate.shape[0]

    def total(part):
        return sum(arrived[j, part * step : (part + 1) * step].astype(F32) for j in range(NX))

    gate[...] = total(0).astype(BF)
    up[...] = total(1).astype(BF)
    down[...] = total(2).T.astype(BF)
    mark[...] = jnp.zeros_like(mark)


def sums(arrived):
    _, rows, hidden = arrived.shape
    step = rows // 3
    return pl.pallas_call(
        sum_kernel,
        out_shape=[bf16(step, hidden)] * 2 + [bf16(hidden, step), MARK],
        in_specs=whole(),
        out_specs=whole(4),
        compiler_params=params(),
        cost_estimate=TINY,
        name="sums",
    )(arrived)


def on_device(tokens, expert_ids, combine_w, w_gate, w_up, w_down, grad_out):
    top, width = expert_ids.shape[1], tokens.shape[1]
    own = prep(tokens, grad_out, expert_ids.T, combine_w.T)
    blocks = {0: (own,)}
    up = down = own
    for r in range(1, NZ // 2):
        up, down = along_z(up, 1), along_z(down, -1)
        blocks[-r], blocks[r] = (up,), (down,)
    up, down = halves(up, down, width + META, [w_up, w_down])
    blocks[NZ // 2] = (along_z(up, 1), along_z(down, -1))

    weights = (w_gate, w_up, w_down)
    tables, back = [], {}
    arrived = []
    for chunk in CHUNKS:
        p, t = pack([blocks[o] for o in chunk], top, width, TINY)
        tables.append(t)
        arrived.append([along_y(p[k], k) for k in range(NY)])

    def outputs(n, h, cost_estimate, after=()):
        mine = [offs for m, offs in BACK if m == n]
        places = [tuple(k * len(CHUNKS[n]) + CHUNKS[n].index(o) for o in offs) for offs in mine for k in range(NY)]
        *out, mark = rows_of(tuple(places), *h, *weights, cost_estimate, after)
        for i, offs in enumerate(mine):
            back[offs] = [along_y(out[i * NY + k], -k) for k in range(NY)]
        return mark

    *h0, rows0 = hidden_of(arrived[0], *weights)
    other, mark_other = grads(1, [rows0], [h0], [])
    own_grads, mark_own = grads(0, [rows0], [h0], [])
    *h1, rows1 = hidden_of(arrived[1], *weights, [mark_other, mark_own])
    mark = outputs(1, h1, TINY)
    other, _ = grads(1, [rows1], [h1], [other], [mark])
    received = lax.ppermute(other, "dp", PERM_CORE)
    mark = outputs(0, h0, SHORT, [mark])

    def returned(n, after=()):
        chunk, offs = BACK[n]
        picked = tuple(CHUNKS[chunk].index(o) for o in offs)
        split = (offs.index(half),) if half in offs else ()
        return zip(offs, unpack(tables[chunk], picked, back[offs], split, SHORT if n else TINY, after))

    half = NZ // 2
    own_grads, grads_done = grads(0, [rows1], [h1], [own_grads, received], [mark])
    grad_gate, grad_up, grad_down, mark = sums(
        lax.all_to_all(own_grads, "dp", split_axis=0, concat_axis=0, tiled=True, axis_index_groups=GROUPS_X)
    )
    parts = dict(returned(0, [grads_done]))
    parts.update(returned(1))
    parts.update(returned(2))
    far_mixed, far_toks = parts[half]
    up, down = along_z(far_mixed, 1), along_z(far_toks, -1)
    up, down = add([(parts[half - 1][0], [(up, 0)]), (parts[1 - half][0], [(down, width)])], LONG)
    for r in range(half - 2, 0, -1):
        up, down = along_z(up, 1), along_z(down, -1)
        up, down = add([(parts[r][0], [(up, 0)]), (parts[-r][0], [(down, 0)])], TINY)
    up, down = along_z(up, 1), along_z(down, -1)
    mixed, grad_tokens = last(parts[0][0], up, down, mark)
    return (mixed, grad_tokens, grad_gate[None], grad_up[None], grad_down[None])


def solution(mesh):
    tok = P(("dp", "expert"), None)
    weight = P("expert", None, None)
    return jax.shard_map(
        on_device,
        mesh=mesh,
        in_specs=(tok, tok, tok, weight, weight, weight, tok),
        out_specs=(tok, tok, P("expert", "dp", None), P("expert", "dp", None), P("expert", None, "dp")),
        check_vma=False,
    )
```

```python
import functools

import jax
import jax.numpy as jnp
from jax import lax
from jax.experimental import pallas as pl
from jax.experimental.pallas import tpu as pltpu
from jax.sharding import PartitionSpec as P

BF = jnp.bfloat16
F32 = jnp.float32

NZ, NY = 8, 4
NX, NC = 4, 2
CAP = 16
LANES = NY * CAP
META = 128
CHUNKS = ((0, 1, -1, 2, -2), (3, -3, 4))
BACK = ((1, (4, 3, -3)), (0, (2, -2)), (0, (1, -1, 0)))
VMEM_LIMIT = 12 * 1024 * 1024


def perm_z(k):
    return [(NY * z + y, NY * ((z + k) % NZ) + y) for z in range(NZ) for y in range(NY)]


def perm_y(k):
    return [(NY * z + y, NY * z + (y + k) % NY) for z in range(NZ) for y in range(NY)]


def perm_x(k):
    return [(NC * x + c, NC * ((x + k) % NX) + c) for x in range(NX) for c in range(NC)]


GROUPS_X = [[NC * x + c for x in range(NX)] for c in range(NC)]
PERM_CORE = [(NC * x + c, NC * x + 1 - c) for x in range(NX) for c in range(NC)]


def along_z(value, k):
    return lax.ppermute(value, "expert", perm_z(k))


def along_y(value, k):
    return lax.ppermute(value, "expert", perm_y(k)) if k % NY else value


def whole(n=1):
    return [pl.BlockSpec(memory_space=pltpu.VMEM)] * n


def params(limit=VMEM_LIMIT):
    return pltpu.CompilerParams(vmem_limit_bytes=limit)


SHORT = pl.CostEstimate(flops=3000000000, bytes_accessed=1, transcendentals=0)
TINY = pl.CostEstimate(flops=1, bytes_accessed=1, transcendentals=0)
LONG = pl.CostEstimate(flops=20000000000, bytes_accessed=1, transcendentals=0)


def unread(n):
    return [pl.BlockSpec(memory_space=pl.ANY)] * n


def bf16(*shape):
    return jax.ShapeDtypeStruct(shape, BF)


MARK = jax.ShapeDtypeStruct((8, 128), F32)


def tn(a, b):
    return lax.dot_general(a, b, (((0,), (0,)), ((), ())), preferred_element_type=F32)


def nt(a, b):
    return lax.dot_general(a, b, (((1,), (1,)), ((), ())), preferred_element_type=F32)


def nn(a, b):
    return jnp.dot(a, b, preferred_element_type=F32)


def prep_kernel(x_ref, g_ref, ids_ref, comb_ref, out_ref):
    tok, width = x_ref.shape
    top = ids_ref.shape[0]
    c = comb_ref[...]
    hi = c.astype(BF).astype(F32)
    rows = jnp.concatenate(
        [ids_ref[...].astype(F32), hi, c - hi, jnp.zeros((META - 3 * top, tok), F32)], axis=0
    )
    rows = jnp.concatenate([rows, jnp.zeros((META, META - tok), F32)], axis=1)
    out_ref[:, :width] = x_ref[...]
    out_ref[:, width : width + META] = rows.T[:tok].astype(BF)
    out_ref[:, width + META :] = g_ref[...]


def prep(tokens, grad_out, ids_t, comb_t):
    tok, width = tokens.shape
    args = (tokens, grad_out, ids_t, comb_t)
    return pl.pallas_call(
        prep_kernel,
        grid=(1,),
        out_shape=bf16(tok, 2 * width + META),
        in_specs=[pl.BlockSpec(a.shape, lambda i: (0, 0)) for a in args],
        out_specs=pl.BlockSpec((tok, 2 * width + META), lambda i: (0, 0)),
        compiler_params=params(60 * 1024 * 1024),
        cost_estimate=TINY,
        name="prep",
    )(*args)


def halves_kernel(up, down, *refs):
    x_ref, g_ref = refs[-2:]
    width = x_ref.shape[1]
    x_ref[...] = up[:, :width]
    g_ref[...] = down[:, width:]


def halves(up, down, width, after):
    tok, full = up.shape
    return pl.pallas_call(
        halves_kernel,
        out_shape=[bf16(tok, width), bf16(tok, full - width)],
        in_specs=whole(2) + unread(len(after)),
        out_specs=whole(2),
        compiler_params=params(),
        cost_estimate=TINY,
        name="halves",
    )(up, down, *after)


def passed_kernel(up, down, *refs):
    refs[-2][...] = up[...]
    refs[-1][...] = down[...]


def passed(up, down, after):
    return pl.pallas_call(
        passed_kernel,
        out_shape=[bf16(*up.shape)] * 2,
        in_specs=whole(2) + unread(len(after)),
        out_specs=whole(2),
        compiler_params=params(),
        cost_estimate=TINY,
        name="passed",
    )(up, down, *after)


def pack_kernel(arity, top, before, *refs):
    refs = list(refs)
    sources = [[refs.pop(0) for _ in range(a)] for a in arity]
    first, refs = refs[: NY if before else 0], refs[NY if before else 0 :]
    outs, (sel_ref, mix_ref) = refs[:NY], refs[NY:]
    for done, out in zip(first, outs):
        out[: before * CAP] = done[...]
    tok = sources[0][0].shape[0]
    width = (outs[0].shape[1]) // 2
    me = lax.axis_index("expert")
    lane_y = (me % NY + lax.broadcasted_iota(jnp.int32, (1, LANES), 1) // CAP) % NY
    lane_e = (me - me % NY + lane_y).astype(F32)
    slot = (lax.broadcasted_iota(jnp.int32, (tok, LANES), 1) % CAP).astype(F32)
    earlier = lax.broadcasted_iota(jnp.int32, (tok, tok), 0) > lax.broadcasted_iota(jnp.int32, (tok, tok), 1)
    earlier = jnp.where(earlier, 1.0, 0.0).astype(BF)
    for i, refs_i in enumerate(sources):
        x_ref = refs_i[0]
        g = refs_i[1][...] if len(refs_i) > 1 else x_ref[:, width + META :]
        meta = x_ref[:, width : width + META].astype(F32)
        chosen = jnp.zeros((tok, LANES), F32)
        hi = jnp.zeros((tok, LANES), F32)
        lo = jnp.zeros((tok, LANES), F32)
        for j in range(top):
            hit = meta[:, j : j + 1] == lane_e
            chosen = jnp.where(hit, 1.0, chosen)
            hi = jnp.where(hit, meta[:, top + j : top + j + 1], hi)
            lo = jnp.where(hit, meta[:, 2 * top + j : 2 * top + j + 1], lo)
        here = nn(earlier, chosen.astype(BF)) == slot
        sel = jnp.where(here, chosen, 0.0).astype(BF)
        hi = jnp.where(here, hi, 0.0).astype(BF)
        lo = jnp.where(here, lo, 0.0).astype(BF)
        sel_ref[i] = sel
        mix_ref[i] = jnp.concatenate([hi, lo], axis=1)
        rows = tn(sel, x_ref[:, :width]).astype(BF)
        cots = (tn(hi, g) + tn(lo, g)).astype(BF)
        for k in range(NY):
            at = (before + i) * CAP
            outs[k][at : at + CAP, :width] = rows[k * CAP : (k + 1) * CAP]
            outs[k][at : at + CAP, width:] = cots[k * CAP : (k + 1) * CAP]


def pack(blocks, top, width, cost_estimate, first=()):
    n, before = len(blocks), first[0].shape[0] // CAP if first else 0
    tok = blocks[0][0].shape[0]
    flat = [a for b in blocks for a in b]
    out = pl.pallas_call(
        functools.partial(pack_kernel, tuple(len(b) for b in blocks), top, before),
        out_shape=[jax.ShapeDtypeStruct(((before + n) * CAP, 2 * width), BF)] * NY
        + [jax.ShapeDtypeStruct((n, tok, LANES), BF), jax.ShapeDtypeStruct((n, tok, 2 * LANES), BF)],
        in_specs=whole(len(flat) + len(first)),
        out_specs=whole(NY + 2),
        compiler_params=params(),
        cost_estimate=cost_estimate,
        name="pack",
    )(*flat, *first)
    return out[:NY], out[NY:]


def unpack_kernel(picked, split, later, sel_ref, mix_ref, *refs):
    rows, outs = refs[:NY], list(refs[NY + later :])
    width = rows[0].shape[1] // 2
    for n, i in enumerate(picked):
        mine = jnp.concatenate([r[n * CAP : (n + 1) * CAP] for r in rows], axis=0)
        out, d_row = mine[:, :width], mine[:, width:]
        mixed = nn(mix_ref[i], jnp.concatenate([out, out], axis=0)).astype(BF)
        toks = nn(sel_ref[i], d_row).astype(BF)
        if n in split:
            outs.pop(0)[...] = mixed
            outs.pop(0)[...] = toks
        else:
            ref = outs.pop(0)
            ref[:, :width] = mixed
            ref[:, width:] = toks


def unpack(tables, picked, rows, split, cost_estimate, after=()):
    sel, mix = tables
    tok, width = sel.shape[1], rows[0].shape[1] // 2
    shapes = []
    for n in range(len(picked)):
        shapes += [bf16(tok, width)] * 2 if n in split else [bf16(tok, 2 * width)]
    out = pl.pallas_call(
        functools.partial(unpack_kernel, picked, split, len(after)),
        out_shape=shapes,
        in_specs=whole(2 + NY) + unread(len(after)),
        out_specs=whole(len(shapes)),
        compiler_params=params(),
        cost_estimate=cost_estimate,
        name="unpack",
    )(sel, mix, *rows, *after)
    out = list(out)
    return [(out.pop(0), out.pop(0)) if n in split else (out.pop(0),) for n in range(len(picked))]


def add_kernel(jobs, later, *refs):
    refs = list(refs)
    ins = [(refs.pop(0), [refs.pop(0) for _ in offs]) for offs in jobs]
    refs = refs[later:]
    step = 256
    for (base, adds), offs, out in zip(ins, jobs, refs):
        for at in range(0, base.shape[1], step):
            total = base[:, at : at + step].astype(F32)
            for a, off in zip(adds, offs):
                if off <= at < off + a.shape[1]:
                    total = total + a[:, at - off : at - off + step].astype(F32)
            out[:, at : at + step] = total.astype(BF)


def add(jobs, cost_estimate, after=()):
    args, offs = [], []
    for base, adds in jobs:
        args += [base, *[a for a, _ in adds]]
        offs.append(tuple(o for _, o in adds))
    return pl.pallas_call(
        functools.partial(add_kernel, tuple(offs), len(after)),
        out_shape=[bf16(*b.shape) for b, _ in jobs],
        in_specs=whole(len(args)) + unread(len(after)),
        out_specs=whole(len(jobs)),
        compiler_params=params(),
        cost_estimate=cost_estimate,
        name="add",
    )(*args, *after)


def last_kernel(base, up, down, mark, mixed, toks):
    width = mixed.shape[1]
    total = base[...].astype(F32) + up[...].astype(F32) + down[...].astype(F32)
    mixed[...] = total[:, :width].astype(BF)
    toks[...] = total[:, width:].astype(BF)


def last(base, up, down, mark):
    tok, width = base.shape
    return pl.pallas_call(
        last_kernel,
        out_shape=[bf16(tok, width // 2)] * 2,
        in_specs=whole(3) + unread(1),
        out_specs=whole(2),
        compiler_params=params(),
        cost_estimate=TINY,
        name="last",
    )(base, up, down, mark)


def hidden_kernel(nb, later, *refs):
    xs, (wg, wu, wd) = refs[:nb], refs[nb : nb + 3]
    hid_ref, dg_ref, du_ref, rows = refs[nb + 3 + later :]
    at = 0
    for r in xs:
        rows[at : at + r.shape[0]] = r[...]
        at += r.shape[0]
    _, width, hidden = wg.shape
    tile = 256
    for h in range(0, hidden, tile):
        cols = slice(h, h + tile)
        x = rows[:, :width]
        gate = nn(x, wg[0, :, cols])
        upper = nn(x, wu[0, :, cols])
        d_hidden = nt(rows[:, width:], wd[0, cols, :])
        s = jax.nn.sigmoid(gate)
        silu = gate * s
        hid_ref[:, cols] = (silu * upper).astype(BF)
        dg_ref[:, cols] = (d_hidden * upper * s * (1.0 + gate * (1.0 - s))).astype(BF)
        du_ref[:, cols] = (d_hidden * silu).astype(BF)


def hidden_of(xs, wg, wu, wd, after=()):
    rows = sum(x.shape[0] for x in xs)
    hidden = wg.shape[2]
    return pl.pallas_call(
        functools.partial(hidden_kernel, len(xs), len(after)),
        out_shape=[jax.ShapeDtypeStruct((rows, hidden), BF)] * 3 + [jax.ShapeDtypeStruct((rows, xs[0].shape[1]), BF)],
        in_specs=whole(len(xs) + 3) + unread(len(after)),
        out_specs=whole(4),
        compiler_params=params(),
        cost_estimate=TINY,
        name="hidden",
    )(*xs, wg, wu, wd, *after)


def rows_kernel(places, later, hid, dg, du, wg, wu, wd, *outs):
    outs = outs[later:]
    outs[-1][...] = jnp.zeros_like(outs[-1])
    _, width, hidden = wg.shape
    tile = 512
    for n in range(0, width, tile):
        cols = slice(n, n + tile)
        out = nn(hid[...], wd[0, :, cols]).astype(BF)
        d_row = (nt(dg[...], wg[0, cols, :]) + nt(du[...], wu[0, cols, :])).astype(BF)
        for r, at in zip(outs, places):
            for i, p in enumerate(at):
                r[i * CAP : (i + 1) * CAP, cols] = out[p * CAP : (p + 1) * CAP]
                r[i * CAP : (i + 1) * CAP, width + n : width + n + tile] = d_row[p * CAP : (p + 1) * CAP]


def rows_of(places, hid, dg, du, wg, wu, wd, cost_estimate, after=()):
    width = wg.shape[1]
    out = [bf16(len(at) * CAP, 2 * width) for at in places]
    return pl.pallas_call(
        functools.partial(rows_kernel, places, len(after)),
        out_shape=out + [MARK],
        in_specs=whole(6) + unread(len(after)),
        out_specs=whole(len(out) + 1),
        compiler_params=params(),
        cost_estimate=cost_estimate,
        name="rows",
    )(hid, dg, du, wg, wu, wd, *after)


def grad_kernel(nc, na, later, other, *refs):
    refs = list(refs)
    rows = [refs.pop(0) for _ in range(nc)]
    hid, dg, du = ([refs.pop(0) for _ in range(nc)] for _ in range(3))
    adds = [refs.pop(0) for _ in range(na)]
    out, mark = refs[later:]
    width = rows[0].shape[1] // 2
    step = out.shape[1] // 3
    core = (lax.axis_index("dp") + other) % NC

    def joined(refs, first=None):
        cols = slice(None) if first is None else pl.ds(pl.multiple_of(first, step), step)
        return jnp.concatenate([r[:, cols] for r in refs], axis=0)

    for j in range(NX):
        at = (NC * j + core) * step
        x, c = joined(rows, at), joined(rows, width + at)
        for i, (a, d) in enumerate(((x, dg), (x, du), (c, hid))):
            value = tn(a, joined(d))
            part = slice(i * step, (i + 1) * step)
            for add in adds:
                value = value + add[j, part, :].astype(F32)
            out[j, part, :] = value.astype(BF)
    mark[...] = jnp.zeros_like(mark)


def grads(other, rows, hids, received, after=()):
    hidden = hids[0][0].shape[1]
    step = rows[0].shape[1] // (2 * NX * NC)
    flat = [h[i] for i in range(3) for h in hids]
    return pl.pallas_call(
        functools.partial(grad_kernel, len(rows), len(received), len(after), other),
        out_shape=[bf16(NX, 3 * step, hidden), MARK],
        in_specs=whole(len(rows) + len(flat) + len(received)) + unread(len(after)),
        out_specs=whole(2),
        compiler_params=params(),
        cost_estimate=TINY,
        name="grads",
    )(*rows, *flat, *received, *after)


def sum_kernel(arrived, gate, up, down, mark):
    step = gate.shape[0]

    def total(part):
        return sum(arrived[j, part * step : (part + 1) * step].astype(F32) for j in range(NX))

    gate[...] = total(0).astype(BF)
    up[...] = total(1).astype(BF)
    down[...] = total(2).T.astype(BF)
    mark[...] = jnp.zeros_like(mark)


def sums(arrived):
    _, rows, hidden = arrived.shape
    step = rows // 3
    return pl.pallas_call(
        sum_kernel,
        out_shape=[bf16(step, hidden)] * 2 + [bf16(hidden, step), MARK],
        in_specs=whole(),
        out_specs=whole(4),
        compiler_params=params(),
        cost_estimate=TINY,
        name="sums",
    )(arrived)


def on_device(tokens, expert_ids, combine_w, w_gate, w_up, w_down, grad_out):
    top, width = expert_ids.shape[1], tokens.shape[1]
    own = prep(tokens, grad_out, expert_ids.T, combine_w.T)
    blocks = {0: (own,)}
    up = down = own
    near = CHUNKS[0][:3]
    for r in range(1, NZ // 2):
        up, down = along_z(up, 1), along_z(down, -1)
        blocks[-r], blocks[r] = (up,), (down,)
        if r == 1:
            first, t0 = pack([blocks[o] for o in near], top, width, TINY)
        if r == 2:
            up, down = passed(up, down, t0[:1])
    p, t1 = pack([blocks[o] for o in CHUNKS[0][3:]], top, width, TINY, first)
    up, down = halves(up, down, width + META, [w_up, w_down])
    blocks[NZ // 2] = (along_z(up, 1), along_z(down, -1))

    weights = (w_gate, w_up, w_down)
    back = {}
    arrived = [[along_y(p[k], k) for k in range(NY)]]
    p, t2 = pack([blocks[o] for o in CHUNKS[1]], top, width, TINY)
    arrived.append([along_y(p[k], k) for k in range(NY)])
    tables = {o: (t0, i) for i, o in enumerate(near)}
    tables.update({o: (t1, i) for i, o in enumerate(CHUNKS[0][3:])})
    tables.update({o: (t2, i) for i, o in enumerate(CHUNKS[1])})

    def outputs(n, h, cost_estimate, after=()):
        mine = [offs for m, offs in BACK if m == n]
        places = [tuple(k * len(CHUNKS[n]) + CHUNKS[n].index(o) for o in offs) for offs in mine for k in range(NY)]
        *out, mark = rows_of(tuple(places), *h, *weights, cost_estimate, after)
        for i, offs in enumerate(mine):
            back[offs] = [along_y(out[i * NY + k], -k) for k in range(NY)]
        return mark

    *h0, rows0 = hidden_of(arrived[0], *weights)
    other, mark_other = grads(1, [rows0], [h0], [])
    own_grads, mark_own = grads(0, [rows0], [h0], [])
    *h1, rows1 = hidden_of(arrived[1], *weights, [mark_other, mark_own])
    mark = outputs(1, h1, TINY)
    other, _ = grads(1, [rows1], [h1], [other])
    received = lax.ppermute(other, "dp", PERM_CORE)
    mark = outputs(0, h0, SHORT, [mark])

    def returned(n, after=()):
        offs = BACK[n][1]
        picked = tuple(tables[o][1] for o in offs)
        split = (offs.index(half),) if half in offs else ()
        cost_estimate = SHORT if n else TINY
        return zip(offs, unpack(tables[offs[0]][0], picked, back[offs], split, cost_estimate, after))

    half = NZ // 2
    own_grads, grads_done = grads(0, [rows1], [h1], [own_grads, received], [mark])
    grad_gate, grad_up, grad_down, mark = sums(
        lax.all_to_all(own_grads, "dp", split_axis=0, concat_axis=0, tiled=True, axis_index_groups=GROUPS_X)
    )
    parts = dict(returned(0, [grads_done]))
    parts.update(returned(1))
    parts.update(returned(2))
    far_mixed, far_toks = parts[half]
    up, down = along_z(far_mixed, 1), along_z(far_toks, -1)
    up, down = add([(parts[half - 1][0], [(up, 0)]), (parts[1 - half][0], [(down, width)])], LONG)
    for r in range(half - 2, 0, -1):
        up, down = along_z(up, 1), along_z(down, -1)
        up, down = add([(parts[r][0], [(up, 0)]), (parts[-r][0], [(down, 0)])], TINY)
    up, down = along_z(up, 1), along_z(down, -1)
    mixed, grad_tokens = last(parts[0][0], up, down, mark)
    return (mixed, grad_tokens, grad_gate[None], grad_up[None], grad_down[None])


def solution(mesh):
    tok = P(("dp", "expert"), None)
    weight = P("expert", None, None)
    return jax.shard_map(
        on_device,
        mesh=mesh,
        in_specs=(tok, tok, tok, weight, weight, weight, tok),
        out_specs=(tok, tok, P("expert", "dp", None), P("expert", "dp", None), P("expert", None, "dp")),
        check_vma=False,
    )
```

```python
import functools

import jax
import jax.numpy as jnp
from jax import lax
from jax.experimental import pallas as pl
from jax.experimental.pallas import tpu as pltpu
from jax.sharding import PartitionSpec as P

BF = jnp.bfloat16
F32 = jnp.float32

NZ, NY = 8, 4
NX, NC = 4, 2
CAP = 16
LANES = NY * CAP
META = 128
CHUNKS = ((0, 1, -1, 2, -2), (3, -3, 4))
BACK = ((1, (4, 3, -3)), (0, (2, -2)), (0, (1, -1, 0)))
VMEM_LIMIT = 12 * 1024 * 1024


def perm_z(k):
    return [(NY * z + y, NY * ((z + k) % NZ) + y) for z in range(NZ) for y in range(NY)]


def perm_y(k):
    return [(NY * z + y, NY * z + (y + k) % NY) for z in range(NZ) for y in range(NY)]


def perm_x(k):
    return [(NC * x + c, NC * ((x + k) % NX) + c) for x in range(NX) for c in range(NC)]


GROUPS_X = [[NC * x + c for x in range(NX)] for c in range(NC)]
PERM_CORE = [(NC * x + c, NC * x + 1 - c) for x in range(NX) for c in range(NC)]


def along_z(value, k):
    return lax.ppermute(value, "expert", perm_z(k))


def along_y(value, k):
    return lax.ppermute(value, "expert", perm_y(k)) if k % NY else value


def whole(n=1):
    return [pl.BlockSpec(memory_space=pltpu.VMEM)] * n


def params(limit=VMEM_LIMIT):
    return pltpu.CompilerParams(vmem_limit_bytes=limit)


SHORT = pl.CostEstimate(flops=3000000000, bytes_accessed=1, transcendentals=0)
TINY = pl.CostEstimate(flops=1, bytes_accessed=1, transcendentals=0)
LONG = pl.CostEstimate(flops=20000000000, bytes_accessed=1, transcendentals=0)


def unread(n):
    return [pl.BlockSpec(memory_space=pl.ANY)] * n


def bf16(*shape):
    return jax.ShapeDtypeStruct(shape, BF)


MARK = jax.ShapeDtypeStruct((8, 128), F32)


def tn(a, b):
    return lax.dot_general(a, b, (((0,), (0,)), ((), ())), preferred_element_type=F32)


def nt(a, b):
    return lax.dot_general(a, b, (((1,), (1,)), ((), ())), preferred_element_type=F32)


def nn(a, b):
    return jnp.dot(a, b, preferred_element_type=F32)


def prep_kernel(x_ref, g_ref, ids_ref, comb_ref, out_ref):
    tok, width = x_ref.shape
    top = ids_ref.shape[0]
    c = comb_ref[...]
    hi = c.astype(BF).astype(F32)
    rows = jnp.concatenate(
        [ids_ref[...].astype(F32), hi, c - hi, jnp.zeros((META - 3 * top, tok), F32)], axis=0
    )
    rows = jnp.concatenate([rows, jnp.zeros((META, META - tok), F32)], axis=1)
    out_ref[:, :width] = x_ref[...]
    out_ref[:, width : width + META] = rows.T[:tok].astype(BF)
    out_ref[:, width + META :] = g_ref[...]


def prep(tokens, grad_out, ids_t, comb_t):
    tok, width = tokens.shape
    args = (tokens, grad_out, ids_t, comb_t)
    return pl.pallas_call(
        prep_kernel,
        grid=(1,),
        out_shape=bf16(tok, 2 * width + META),
        in_specs=[pl.BlockSpec(a.shape, lambda i: (0, 0)) for a in args],
        out_specs=pl.BlockSpec((tok, 2 * width + META), lambda i: (0, 0)),
        compiler_params=params(60 * 1024 * 1024),
        cost_estimate=TINY,
        name="prep",
    )(*args)


def halves_kernel(up, down, *refs):
    x_ref, g_ref = refs[-2:]
    width = x_ref.shape[1]
    x_ref[...] = up[:, :width]
    g_ref[...] = down[:, width:]


def halves(up, down, width, after):
    tok, full = up.shape
    return pl.pallas_call(
        halves_kernel,
        out_shape=[bf16(tok, width), bf16(tok, full - width)],
        in_specs=whole(2) + unread(len(after)),
        out_specs=whole(2),
        compiler_params=params(),
        cost_estimate=TINY,
        name="halves",
    )(up, down, *after)


def passed_kernel(up, down, *refs):
    refs[-2][...] = up[...]
    refs[-1][...] = down[...]


def passed(up, down, after):
    return pl.pallas_call(
        passed_kernel,
        out_shape=[bf16(*up.shape)] * 2,
        in_specs=whole(2) + unread(len(after)),
        out_specs=whole(2),
        compiler_params=params(),
        cost_estimate=TINY,
        name="passed",
    )(up, down, *after)


def routing(block, width, top):
    tok = block.shape[0]
    me = lax.axis_index("expert")
    lane_y = (me % NY + lax.broadcasted_iota(jnp.int32, (1, LANES), 1) // CAP) % NY
    lane_e = (me - me % NY + lane_y).astype(F32)
    slot = (lax.broadcasted_iota(jnp.int32, (tok, LANES), 1) % CAP).astype(F32)
    earlier = lax.broadcasted_iota(jnp.int32, (tok, tok), 0) > lax.broadcasted_iota(jnp.int32, (tok, tok), 1)
    earlier = jnp.where(earlier, 1.0, 0.0).astype(BF)
    meta = block[:, width : width + META].astype(F32)
    chosen = jnp.zeros((tok, LANES), F32)
    hi = jnp.zeros((tok, LANES), F32)
    lo = jnp.zeros((tok, LANES), F32)
    for j in range(top):
        hit = meta[:, j : j + 1] == lane_e
        chosen = jnp.where(hit, 1.0, chosen)
        hi = jnp.where(hit, meta[:, top + j : top + j + 1], hi)
        lo = jnp.where(hit, meta[:, 2 * top + j : 2 * top + j + 1], lo)
    here = nn(earlier, chosen.astype(BF)) == slot
    return tuple(jnp.where(here, v, 0.0).astype(BF) for v in (chosen, hi, lo))


def tables_kernel(n, top, *refs):
    sel_ref, mix_ref = refs[-2:]
    for i in range(n):
        sel, hi, lo = routing(refs[i], (refs[i].shape[1] - META) // 2, top)
        sel_ref[i] = sel
        mix_ref[i] = jnp.concatenate([hi, lo], axis=1)


def table_shapes(n, tok):
    return [bf16(n, tok, LANES), bf16(n, tok, 2 * LANES)]


def tables_of(blocks, top, after):
    n, tok = len(blocks), blocks[0].shape[0]
    return pl.pallas_call(
        functools.partial(tables_kernel, n, top),
        out_shape=table_shapes(n, tok),
        in_specs=whole(n) + unread(len(after)),
        out_specs=whole(2),
        compiler_params=params(),
        cost_estimate=TINY,
        name="tables",
    )(*blocks, *after)


def pack_kernel(arity, top, before, *refs):
    refs = list(refs)
    sources = [[refs.pop(0) for _ in range(a)] for a in arity]
    first, refs = refs[: NY if before else 0], refs[NY if before else 0 :]
    outs, tables = refs[:NY], refs[NY:]
    for done, out in zip(first, outs):
        out[: before * CAP] = done[...]
    width = (outs[0].shape[1]) // 2
    for i, refs_i in enumerate(sources):
        x_ref = refs_i[0]
        g = refs_i[1][...] if len(refs_i) > 1 else x_ref[:, width + META :]
        sel, hi, lo = routing(x_ref, width, top)
        if tables:
            tables[0][i] = sel
            tables[1][i] = jnp.concatenate([hi, lo], axis=1)
        rows = tn(sel, x_ref[:, :width]).astype(BF)
        cots = (tn(hi, g) + tn(lo, g)).astype(BF)
        for k in range(NY):
            at = (before + i) * CAP
            outs[k][at : at + CAP, :width] = rows[k * CAP : (k + 1) * CAP]
            outs[k][at : at + CAP, width:] = cots[k * CAP : (k + 1) * CAP]


def pack(blocks, top, width, cost_estimate, first=()):
    n, before = len(blocks), first[0].shape[0] // CAP if first else 0
    tok = blocks[0][0].shape[0]
    flat = [a for b in blocks for a in b]
    tables = [] if first else table_shapes(n, tok)
    out = pl.pallas_call(
        functools.partial(pack_kernel, tuple(len(b) for b in blocks), top, before),
        out_shape=[bf16((before + n) * CAP, 2 * width)] * NY + tables,
        in_specs=whole(len(flat) + len(first)),
        out_specs=whole(NY + len(tables)),
        compiler_params=params(),
        cost_estimate=cost_estimate,
        name="pack",
    )(*flat, *first)
    return out[:NY], out[NY:]


def unpack_kernel(picked, split, later, sel_ref, mix_ref, *refs):
    rows, outs = refs[:NY], list(refs[NY + later :])
    width = rows[0].shape[1] // 2
    for n, i in enumerate(picked):
        mine = jnp.concatenate([r[n * CAP : (n + 1) * CAP] for r in rows], axis=0)
        out, d_row = mine[:, :width], mine[:, width:]
        mixed = nn(mix_ref[i], jnp.concatenate([out, out], axis=0)).astype(BF)
        toks = nn(sel_ref[i], d_row).astype(BF)
        if n in split:
            outs.pop(0)[...] = mixed
            outs.pop(0)[...] = toks
        else:
            ref = outs.pop(0)
            ref[:, :width] = mixed
            ref[:, width:] = toks


def unpack(tables, picked, rows, split, cost_estimate, after=()):
    sel, mix = tables
    tok, width = sel.shape[1], rows[0].shape[1] // 2
    shapes = []
    for n in range(len(picked)):
        shapes += [bf16(tok, width)] * 2 if n in split else [bf16(tok, 2 * width)]
    out = pl.pallas_call(
        functools.partial(unpack_kernel, picked, split, len(after)),
        out_shape=shapes,
        in_specs=whole(2 + NY) + unread(len(after)),
        out_specs=whole(len(shapes)),
        compiler_params=params(),
        cost_estimate=cost_estimate,
        name="unpack",
    )(sel, mix, *rows, *after)
    out = list(out)
    return [(out.pop(0), out.pop(0)) if n in split else (out.pop(0),) for n in range(len(picked))]


def add_kernel(jobs, later, *refs):
    refs = list(refs)
    ins = [(refs.pop(0), [refs.pop(0) for _ in offs]) for offs in jobs]
    refs = refs[later:]
    step = 256
    for (base, adds), offs, out in zip(ins, jobs, refs):
        for at in range(0, base.shape[1], step):
            total = base[:, at : at + step].astype(F32)
            for a, off in zip(adds, offs):
                if off <= at < off + a.shape[1]:
                    total = total + a[:, at - off : at - off + step].astype(F32)
            out[:, at : at + step] = total.astype(BF)


def add(jobs, cost_estimate, after=()):
    args, offs = [], []
    for base, adds in jobs:
        args += [base, *[a for a, _ in adds]]
        offs.append(tuple(o for _, o in adds))
    return pl.pallas_call(
        functools.partial(add_kernel, tuple(offs), len(after)),
        out_shape=[bf16(*b.shape) for b, _ in jobs],
        in_specs=whole(len(args)) + unread(len(after)),
        out_specs=whole(len(jobs)),
        compiler_params=params(),
        cost_estimate=cost_estimate,
        name="add",
    )(*args, *after)


def last_kernel(base, up, down, mark, mixed, toks):
    width = mixed.shape[1]
    total = base[...].astype(F32) + up[...].astype(F32) + down[...].astype(F32)
    mixed[...] = total[:, :width].astype(BF)
    toks[...] = total[:, width:].astype(BF)


def last(base, up, down, mark):
    tok, width = base.shape
    return pl.pallas_call(
        last_kernel,
        out_shape=[bf16(tok, width // 2)] * 2,
        in_specs=whole(3) + unread(1),
        out_specs=whole(2),
        compiler_params=params(),
        cost_estimate=TINY,
        name="last",
    )(base, up, down, mark)


def hidden_kernel(nb, later, *refs):
    xs, (wg, wu, wd) = refs[:nb], refs[nb : nb + 3]
    hid_ref, dg_ref, du_ref, rows = refs[nb + 3 + later :]
    at = 0
    for r in xs:
        rows[at : at + r.shape[0]] = r[...]
        at += r.shape[0]
    _, width, hidden = wg.shape
    tile = 256
    for h in range(0, hidden, tile):
        cols = slice(h, h + tile)
        x = rows[:, :width]
        gate = nn(x, wg[0, :, cols])
        upper = nn(x, wu[0, :, cols])
        d_hidden = nt(rows[:, width:], wd[0, cols, :])
        s = jax.nn.sigmoid(gate)
        silu = gate * s
        hid_ref[:, cols] = (silu * upper).astype(BF)
        dg_ref[:, cols] = (d_hidden * upper * s * (1.0 + gate * (1.0 - s))).astype(BF)
        du_ref[:, cols] = (d_hidden * silu).astype(BF)


def hidden_of(xs, wg, wu, wd, after=()):
    rows = sum(x.shape[0] for x in xs)
    hidden = wg.shape[2]
    return pl.pallas_call(
        functools.partial(hidden_kernel, len(xs), len(after)),
        out_shape=[jax.ShapeDtypeStruct((rows, hidden), BF)] * 3 + [jax.ShapeDtypeStruct((rows, xs[0].shape[1]), BF)],
        in_specs=whole(len(xs) + 3) + unread(len(after)),
        out_specs=whole(4),
        compiler_params=params(),
        cost_estimate=TINY,
        name="hidden",
    )(*xs, wg, wu, wd, *after)


def rows_kernel(places, later, hid, dg, du, wg, wu, wd, *outs):
    outs = outs[later:]
    outs[-1][...] = jnp.zeros_like(outs[-1])
    _, width, hidden = wg.shape
    tile = 512
    for n in range(0, width, tile):
        cols = slice(n, n + tile)
        out = nn(hid[...], wd[0, :, cols]).astype(BF)
        d_row = (nt(dg[...], wg[0, cols, :]) + nt(du[...], wu[0, cols, :])).astype(BF)
        for r, at in zip(outs, places):
            for i, p in enumerate(at):
                r[i * CAP : (i + 1) * CAP, cols] = out[p * CAP : (p + 1) * CAP]
                r[i * CAP : (i + 1) * CAP, width + n : width + n + tile] = d_row[p * CAP : (p + 1) * CAP]


def rows_of(places, hid, dg, du, wg, wu, wd, cost_estimate, after=()):
    width = wg.shape[1]
    out = [bf16(len(at) * CAP, 2 * width) for at in places]
    return pl.pallas_call(
        functools.partial(rows_kernel, places, len(after)),
        out_shape=out + [MARK],
        in_specs=whole(6) + unread(len(after)),
        out_specs=whole(len(out) + 1),
        compiler_params=params(),
        cost_estimate=cost_estimate,
        name="rows",
    )(hid, dg, du, wg, wu, wd, *after)


def grad_kernel(nc, na, later, other, *refs):
    refs = list(refs)
    rows = [refs.pop(0) for _ in range(nc)]
    hid, dg, du = ([refs.pop(0) for _ in range(nc)] for _ in range(3))
    adds = [refs.pop(0) for _ in range(na)]
    out, mark = refs[later:]
    width = rows[0].shape[1] // 2
    step = out.shape[1] // 3
    core = (lax.axis_index("dp") + other) % NC

    def joined(refs, first=None):
        cols = slice(None) if first is None else pl.ds(pl.multiple_of(first, step), step)
        return jnp.concatenate([r[:, cols] for r in refs], axis=0)

    for j in range(NX):
        at = (NC * j + core) * step
        x, c = joined(rows, at), joined(rows, width + at)
        for i, (a, d) in enumerate(((x, dg), (x, du), (c, hid))):
            value = tn(a, joined(d))
            part = slice(i * step, (i + 1) * step)
            for add in adds:
                value = value + add[j, part, :].astype(F32)
            out[j, part, :] = value.astype(BF)
    mark[...] = jnp.zeros_like(mark)


def grads(other, rows, hids, received, after=()):
    hidden = hids[0][0].shape[1]
    step = rows[0].shape[1] // (2 * NX * NC)
    flat = [h[i] for i in range(3) for h in hids]
    return pl.pallas_call(
        functools.partial(grad_kernel, len(rows), len(received), len(after), other),
        out_shape=[bf16(NX, 3 * step, hidden), MARK],
        in_specs=whole(len(rows) + len(flat) + len(received)) + unread(len(after)),
        out_specs=whole(2),
        compiler_params=params(),
        cost_estimate=TINY,
        name="grads",
    )(*rows, *flat, *received, *after)


def sum_kernel(arrived, gate, up, down, mark):
    step = gate.shape[0]
    tile = 128
    for part, out in enumerate((gate, up, down)):
        for at in range(0, step, tile):
            rows = slice(part * step + at, part * step + at + tile)
            for col in range(0, arrived.shape[2], tile):
                cols = slice(col, col + tile)
                total = sum(arrived[j, rows, cols].astype(F32) for j in range(NX))
                if part == 2:
                    out[cols, at : at + tile] = total.T.astype(BF)
                else:
                    out[at : at + tile, cols] = total.astype(BF)
    mark[...] = jnp.zeros_like(mark)


def sums(arrived):
    _, rows, hidden = arrived.shape
    step = rows // 3
    return pl.pallas_call(
        sum_kernel,
        out_shape=[bf16(step, hidden)] * 2 + [bf16(hidden, step), MARK],
        in_specs=whole(),
        out_specs=whole(4),
        compiler_params=params(),
        cost_estimate=TINY,
        name="sums",
    )(arrived)


def on_device(tokens, expert_ids, combine_w, w_gate, w_up, w_down, grad_out):
    top, width = expert_ids.shape[1], tokens.shape[1]
    own = prep(tokens, grad_out, expert_ids.T, combine_w.T)
    blocks = {0: (own,)}
    up = down = own
    near = CHUNKS[0][:3]
    for r in range(1, NZ // 2):
        up, down = along_z(up, 1), along_z(down, -1)
        blocks[-r], blocks[r] = (up,), (down,)
        if r == 1:
            first, t0 = pack([blocks[o] for o in near], top, width, TINY)
        if r == 2:
            up, down = passed(up, down, t0[:1])
    p, _ = pack([blocks[o] for o in CHUNKS[0][3:]], top, width, TINY, first)
    t1 = tables_of([blocks[o][0] for o in CHUNKS[0][3:]], top, [w_up, w_down])
    up, down = halves(up, down, width + META, [])
    blocks[NZ // 2] = (along_z(up, 1), along_z(down, -1))

    weights = (w_gate, w_up, w_down)
    back = {}
    arrived = [[along_y(p[k], k) for k in range(NY)]]
    p, t2 = pack([blocks[o] for o in CHUNKS[1]], top, width, TINY)
    arrived.append([along_y(p[k], k) for k in range(NY)])
    tables = {o: (t0, i) for i, o in enumerate(near)}
    tables.update({o: (t1, i) for i, o in enumerate(CHUNKS[0][3:])})
    tables.update({o: (t2, i) for i, o in enumerate(CHUNKS[1])})

    def outputs(n, h, cost_estimate, after=()):
        mine = [offs for m, offs in BACK if m == n]
        places = [tuple(k * len(CHUNKS[n]) + CHUNKS[n].index(o) for o in offs) for offs in mine for k in range(NY)]
        *out, mark = rows_of(tuple(places), *h, *weights, cost_estimate, after)
        for i, offs in enumerate(mine):
            back[offs] = [along_y(out[i * NY + k], -k) for k in range(NY)]
        return mark

    *h0, rows0 = hidden_of(arrived[0], *weights, t1[:1])
    other, mark_other = grads(1, [rows0], [h0], [])
    own_grads, mark_own = grads(0, [rows0], [h0], [])
    *h1, rows1 = hidden_of(arrived[1], *weights, [mark_other, mark_own])
    mark = outputs(1, h1, TINY)
    other, _ = grads(1, [rows1], [h1], [other])
    received = lax.ppermute(other, "dp", PERM_CORE)
    mark = outputs(0, h0, SHORT, [mark])

    def returned(n, after=()):
        offs = BACK[n][1]
        picked = tuple(tables[o][1] for o in offs)
        split = (offs.index(half),) if half in offs else ()
        cost_estimate = SHORT if n else TINY
        return zip(offs, unpack(tables[offs[0]][0], picked, back[offs], split, cost_estimate, after))

    half = NZ // 2
    own_grads, grads_done = grads(0, [rows1], [h1], [own_grads, received], [mark])
    grad_gate, grad_up, grad_down, mark = sums(
        lax.all_to_all(own_grads, "dp", split_axis=0, concat_axis=0, tiled=True, axis_index_groups=GROUPS_X)
    )
    parts = dict(returned(0, [grads_done]))
    parts.update(returned(1))
    parts.update(returned(2))
    far_mixed, far_toks = parts[half]
    up, down = along_z(far_mixed, 1), along_z(far_toks, -1)
    up, down = add([(parts[half - 1][0], [(up, 0)]), (parts[1 - half][0], [(down, width)])], LONG)
    for r in range(half - 2, 0, -1):
        up, down = along_z(up, 1), along_z(down, -1)
        up, down = add([(parts[r][0], [(up, 0)]), (parts[-r][0], [(down, 0)])], TINY)
    up, down = along_z(up, 1), along_z(down, -1)
    mixed, grad_tokens = last(parts[0][0], up, down, mark)
    return (mixed, grad_tokens, grad_gate[None], grad_up[None], grad_down[None])


def solution(mesh):
    tok = P(("dp", "expert"), None)
    weight = P("expert", None, None)
    return jax.shard_map(
        on_device,
        mesh=mesh,
        in_specs=(tok, tok, tok, weight, weight, weight, tok),
        out_specs=(tok, tok, P("expert", "dp", None), P("expert", "dp", None), P("expert", None, "dp")),
        check_vma=False,
    )
```
